256 devices in a mesh: sensor: 8 (over z), slab: 32 (over y, x, core).
Axes of the slice: x: 4, y: 4, z: 8, core: 2. Of those that a mesh axis runs over, the one named last changes fastest.
Arguments:
- volume: bfloat16 [32, 256, 4, 512], P('sensor', 'slab'), may hold values from -6 to 6
- measured: bfloat16 [512, 4, 128], P(('sensor', 'slab')), may hold values from -6 to 6
- blocks: bfloat16 [512, 160, 64, 128], P('sensor', 'slab'), may hold values from -0.0625 to 0.0625
- voxel_ids: int32 [512, 160], P('sensor', 'slab'), may hold values from 0 to 2047
- counts: int32 [512, 32], P('sensor', 'slab'), may hold values from 0 to 5, as said below
- exponents: int32 [512, 160], P('sensor', 'slab'), may hold values from -1 to 1
- conv_in: float32 [32, 2, 27], replicated, may hold values from -0.875 to 0.875
- conv_bias: float32 [32], replicated, may hold values from -3 to 3
- conv_out: float32 [32], replicated, may hold values from -1 to 1
Outputs:
- updated: float32 [32, 256, 4, 512], P('sensor', 'slab')
The draws below stay inside these ranges and needn't reach their ends.
Inputs may be any that keep to these rules, and one draw needn't show every extreme that they name: `counts`: every sample block has 5 live slots in at least one slab.
All inputs are finite; a program needn't handle non-finite values.
Results may differ from the reference program's by a relative error of at most 0.006.
Values may be sent and summed in bfloat16 or wider, within the bound.
No kernel may reach another device: no remote copies, remote signals or barrier semaphores. Data moves between devices by JAX's collectives and lax.ppermute only.
A program may use at most 128 MiB of HBM per device.

```python
import jax
import jax.numpy as jnp
from jax import lax

TBLK = 128
VBLK = 64
KPS = 5
CHAN = 32
GZ_DEV = 8
GY = 512
BATCH = 4
GROUP_BLOCKS = 64
ALL_BLOCKS = 512
NX = 32
NZ = 256
SLAB_BLOCKS = 2048
N_SENSOR = 8
N_SLAB = 32


def draw_counts(key, part):
    key = jax.random.fold_in(key, 11)
    first_key, second_key = jax.random.split(key)
    center = jax.random.randint(first_key, (ALL_BLOCKS, 1), 0, N_SLAB)
    slab_iota = jnp.arange(N_SLAB, dtype=jnp.int32)[None, :]
    distance = jnp.abs(slab_iota - center)
    dropped = jax.random.randint(second_key, (ALL_BLOCKS, N_SLAB), 0, 2)
    value = KPS - distance * KPS // N_SLAB - dropped * (distance > 0).astype(jnp.int32)
    return jnp.clip(value, 0, KPS).astype(jnp.int32)


def touch_ends(result, stream_key, smallest, top_value):
    extent = result.shape
    index_at = [jax.random.randint(jax.random.fold_in(stream_key, axis), (), 0, extent[axis]) for axis in range(len(extent))]
    result = result.at[tuple(index_at)].set(smallest)
    longest = extent.index(max(extent))
    index_at[longest] = (index_at[longest] + 1) % extent[longest]
    return result.at[tuple(index_at)].set(top_value)


def shard_levels(rng, shape, shards, smallest, high):
    loudness, own = 1.0, jax.random.fold_in(rng, 6)
    for position, shards_of in shards:
        heights = jnp.exp(jax.random.uniform(jax.random.fold_in(own, position), (shards_of,), jnp.float32, smallest / len(shards), high / len(shards)))
        loudness = loudness * jnp.repeat(heights, shape[position] // shards_of).reshape([-1 if axis == position else 1 for axis in range(len(shape))])
    return loudness


def gaussian(stream_key, dims, width, bound, cuts=(), kind=jnp.bfloat16):
    array = jax.random.normal(stream_key, dims, jnp.float32) * width
    if len(cuts) > 0:
        array = shard_levels(stream_key, dims, cuts, -0.22, 0.18) * array
    return jnp.clip(array, min=-bound, max=bound).astype(kind)


def setup_inputs(seed: int = 0) -> dict:
    keys = jax.random.split(jax.random.key(seed), 10)
    volume = gaussian(keys[0], (NX, NZ, BATCH, GY), 1.0, 6.0, ((0, 8), (1, 32)))
    measured = gaussian(keys[1], (ALL_BLOCKS, BATCH, TBLK), 1.0, 6.0, ((0, 256),))
    blocks = gaussian(keys[2], (ALL_BLOCKS, N_SLAB * KPS, VBLK, TBLK), (VBLK * KPS * N_SLAB) ** -0.5, 0.0625, ((0, 8), (1, 32)))
    voxel_ids = touch_ends(jax.random.randint(keys[3], (ALL_BLOCKS, N_SLAB * KPS), 0, SLAB_BLOCKS), jax.random.fold_in(keys[3], 1), 0, SLAB_BLOCKS - 1).astype(jnp.int32)
    counts = draw_counts(jax.random.fold_in(keys[9], 71), 0)
    exponents = touch_ends(jax.random.randint(keys[5], (ALL_BLOCKS, N_SLAB * KPS), -1, 2), jax.random.fold_in(keys[5], 1), -1, 1).astype(jnp.int32)
    conv_in = gaussian(keys[6], (CHAN, 2, 27), 54 ** -0.5, 0.875, (), jnp.float32)
    conv_bias = gaussian(keys[7], (CHAN,), 0.5, 3.0, (), jnp.float32)
    conv_out = gaussian(keys[8], (CHAN,), CHAN ** -0.5, 1.0, (), jnp.float32)
    return dict(volume=volume, measured=measured, blocks=blocks, voxel_ids=voxel_ids, counts=counts, exponents=exponents, conv_in=conv_in, conv_bias=conv_bias, conv_out=conv_out)


def to_blocks(slab_volume):
    depth, planes, batch_size, cells_y = slab_volume.shape
    reshaped = slab_volume.reshape(depth, planes, batch_size, cells_y // VBLK, VBLK)
    return reshaped.transpose(0, 1, 3, 2, 4).reshape(depth * planes * (cells_y // VBLK), batch_size, VBLK)


def from_blocks(blocked, depth, planes):
    block_count, batch_size, unused = blocked.shape
    halves = block_count // (depth * planes)
    reshaped = blocked.reshape(depth, planes, halves, batch_size, VBLK)
    return reshaped.transpose(0, 1, 3, 2, 4).reshape(depth, planes, batch_size, halves * VBLK)


def slot_weights(live_slots, exponents):
    slot_iota = lax.broadcasted_iota(jnp.int32, exponents.shape, 1)
    scaled = jnp.exp2(exponents.astype(jnp.float32))
    return jnp.where(slot_iota < live_slots[:, None], scaled, jnp.zeros_like(scaled)).astype(jnp.bfloat16)


def convolve(padded, conv_in, conv_bias, conv_out, base_volume):
    depth, planes, batch_size, cells_y = base_volume.shape
    padded = jnp.pad(padded, ((0, 0), (0, 0), (0, 0), (0, 0), (1, 1)))
    patches = jnp.stack([padded[:, shift_x:shift_x + depth, shift_z:shift_z + planes, :, shift_y:shift_y + cells_y]
                         for shift_x in range(3) for shift_z in range(3) for shift_y in range(3)], 1)
    hidden = jnp.einsum('cit,itxzby->cxzby', conv_in, patches, precision=lax.Precision.HIGHEST)
    active = jnp.maximum(hidden + conv_bias[:, None, None, None, None], 0.0)
    return base_volume + jnp.einsum('c,cxzby->xzby', conv_out, active, precision=lax.Precision.HIGHEST)


def reference(volume, measured, blocks, voxel_ids, counts, exponents, conv_in, conv_bias, conv_out):
    def slab_inputs(slab_index):
        slab_volume = lax.dynamic_slice_in_dim(volume, slab_index * GZ_DEV, GZ_DEV, 1)
        slot_ids = lax.dynamic_slice_in_dim(voxel_ids, slab_index * KPS, KPS, 1)
        live_slots = lax.dynamic_slice_in_dim(counts, slab_index, 1, 1)[:, 0]
        weights = slot_weights(live_slots, lax.dynamic_slice_in_dim(exponents, slab_index * KPS, KPS, 1))
        block_rows = lax.dynamic_slice_in_dim(blocks, slab_index * KPS, KPS, 1)
        return slab_volume, slot_ids, weights, block_rows

    def forward(running, slab_index):
        slab_volume, slot_ids, weights, block_rows = slab_inputs(slab_index)
        gathered = to_blocks(slab_volume)[slot_ids] * weights[:, :, None, None]
        contrib = jnp.einsum('skvt,skbv->sbt', block_rows.astype(jnp.float32), gathered.astype(jnp.float32),
                             precision=lax.Precision.HIGHEST)
        return running + contrib, None

    slab_range = jnp.arange(N_SLAB, dtype=jnp.int32)
    projection, unused = lax.scan(forward, jnp.zeros((ALL_BLOCKS, BATCH, TBLK), jnp.float32), slab_range)
    residual = (projection - measured.astype(jnp.float32)).astype(jnp.bfloat16)
    group_of = jnp.arange(ALL_BLOCKS, dtype=jnp.int32) // GROUP_BLOCKS

    def adjoint(slab_index):
        slab_volume, slot_ids, weights, block_rows = slab_inputs(slab_index)
        contrib = jnp.einsum('skvt,sbt->skbv', block_rows.astype(jnp.float32), residual.astype(jnp.float32),
                             precision=lax.Precision.HIGHEST)
        contrib = contrib * weights[:, :, None, None].astype(jnp.float32)
        segment = slot_ids + group_of[:, None] * SLAB_BLOCKS
        summed = jax.ops.segment_sum(contrib.reshape(-1, BATCH, VBLK), segment.reshape(-1), N_SENSOR * SLAB_BLOCKS)
        rounded = lax.optimization_barrier(summed.astype(jnp.bfloat16)).astype(jnp.float32)
        per_slab = jnp.sum(rounded.reshape(N_SENSOR, SLAB_BLOCKS, BATCH, VBLK), axis=0)
        return from_blocks(per_slab, NX, GZ_DEV)

    slab_grads = lax.map(adjoint, slab_range)
    gradient = slab_grads.transpose(1, 0, 2, 3, 4).reshape(NX, NZ, BATCH, GY)
    base_volume = volume.astype(jnp.float32)

    def update_one(volume_index):
        base_one = lax.dynamic_slice_in_dim(base_volume, volume_index, 1, 2)
        grad_one = lax.dynamic_slice_in_dim(gradient, volume_index, 1, 2)
        stacked = jnp.stack([base_one, grad_one], 0)
        padded = jnp.pad(stacked, ((0, 0), (1, 1), (1, 1), (0, 0), (0, 0)))
        return convolve(padded, conv_in, conv_bias, conv_out, base_one)

    results = lax.map(update_one, jnp.arange(BATCH, dtype=jnp.int32))
    return results[:, :, :, 0, :].transpose(1, 2, 0, 3)
```

```python
import functools

import jax
import jax.numpy as jnp
import numpy as np
from jax import lax
from jax.experimental import pallas as pl
from jax.experimental.pallas import tpu as pltpu
from jax.sharding import PartitionSpec as P

F32 = jnp.float32
BF16 = jnp.bfloat16
I32 = jnp.int32

JB = 64
KS = 5
SLOTS = JB * KS
NB = 4
TB = 128
OWN = 256
SHARD_ROWS = OWN + 16
CHAN = 32
TAPS = 192
SPLIT = 144


def vmem():
    return pl.BlockSpec(memory_space=pltpu.VMEM)


def smem():
    return pl.BlockSpec(memory_space=pltpu.SMEM)


def params(mib):
    return pltpu.CompilerParams(vmem_limit_bytes=mib * 1024 * 1024)


def cost(us):
    return pl.CostEstimate(flops=0, bytes_accessed=int(us * 3.0e6), transcendentals=0)


def lower_half(rows):
    return lax.broadcasted_iota(I32, (rows, 128), 1) < 64


def swapped(tile):
    return pltpu.roll(tile, 64, axis=1)


def pair_halves(first, second, low):
    return jnp.where(low, first, swapped(second)), jnp.where(low, swapped(first), second)


def prep_kernel(volume_ref, ids_ref, out_ref, rows):
    for i in range(32):
        image = volume_ref[i // 8, i % 8].astype(F32)
        for q in range(4):
            rows[q, 4 * i : 4 * i + 4, :] = image[:, 128 * q : 128 * q + 128]
    low = lower_half(32)
    for m in range(2):
        for q in range(4):
            one = rows[q, pl.ds(2 * m, 32, stride=4), :]
            two = rows[q, pl.ds(2 * m + 1, 32, stride=4), :]
            even, odd = pair_halves(one, two, low)
            out_ref[64 * q : 64 * q + 32, 128 * m : 128 * m + 128] = even.astype(BF16)
            out_ref[64 * q + 32 : 64 * q + 64, 128 * m : 128 * m + 128] = odd.astype(BF16)
    out_ref[OWN:SHARD_ROWS, :] = ids_ref[...]


def prep(volume, id_rows):
    return pl.pallas_call(
        prep_kernel,
        out_shape=jax.ShapeDtypeStruct((SHARD_ROWS, 256), BF16),
        in_specs=[vmem(), vmem()],
        out_specs=vmem(),
        scratch_shapes=[pltpu.VMEM((4, 128, 128), F32)],
        compiler_params=params(8),
        cost_estimate=cost(1.0),
        name="images_to_rows",
    )(volume, id_rows)


def add_gathered(acc, keys, weights, base, shard):
    lane = lax.broadcasted_iota(I32, (SLOTS, OWN), 1)
    hot = jnp.where(lane == keys - base, weights, 0.0).astype(BF16)
    return acc + jnp.dot(hot, shard, preferred_element_type=F32)


def gather_kernel(base_ref, keys_ref, weights_ref, *refs):
    shards, out_ref = refs[:-1], refs[-1]
    acc = jnp.zeros((SLOTS, 256), F32)
    for i, shard in enumerate(shards):
        acc = add_gathered(acc, keys_ref[...], weights_ref[...], base_ref[i], shard[0:OWN, :])
    out_ref[...] = acc


def gather_first(base, keys, weights, shards):
    return pl.pallas_call(
        gather_kernel,
        out_shape=jax.ShapeDtypeStruct((SLOTS, 256), F32),
        in_specs=[smem()] + [vmem()] * (2 + len(shards)),
        out_specs=vmem(),
        compiler_params=params(16),
        cost_estimate=cost(2.0),
        name="gather_first",
    )(base, keys, weights, *shards)


CHUNKS = 8


def start_blocks(blocks_ref, held, sems):
    step = JB // CHUNKS
    copies = [
        pltpu.make_async_copy(
            blocks_ref.at[pl.ds(c * step, step)], held.at[pl.ds(c * step, step)], sems.at[c]
        )
        for c in range(CHUNKS)
    ]
    for copy in copies:
        copy.start()
    return copies


def project_kernel(
    base_ref,
    slab_ref,
    keys_ref,
    weights_ref,
    before_ref,
    three_ref,
    minus_ref,
    half_a_ref,
    half_b_ref,
    measured_ref,
    blocks_ref,
    out_ref,
    held,
    far,
    lhs,
    total,
    sems,
):
    copies = start_blocks(blocks_ref, held, sems)
    far[0:SPLIT, :] = half_a_ref[...]
    far[SPLIT:SHARD_ROWS, :] = half_b_ref[...]
    acc = before_ref[...]
    keys, weights = keys_ref[...], weights_ref[...]
    for i, shard in enumerate((three_ref, minus_ref, far)):
        acc = add_gathered(acc, keys, weights, base_ref[5 + i], shard[0:OWN, :])
    low = lower_half(JB)
    for m in range(2):
        cols = slice(128 * m, 128 * m + 128)
        for q in range(3):
            one = acc[2 * q * JB : (2 * q + 1) * JB, cols]
            if q < 2:
                two = acc[(2 * q + 1) * JB : (2 * q + 2) * JB, cols]
                even, odd = pair_halves(one, two, low)
            else:
                even, odd = one, swapped(one)
            lhs[q, pl.ds(2 * m, JB, stride=4), :] = even
            lhs[q, pl.ds(2 * m + 1, JB, stride=4), :] = odd
    upper = lax.broadcasted_iota(I32, (8, TB), 0) < 4
    for c in range(CHUNKS):
        copies[c].wait()
        for p in range(c * (JB // CHUNKS) // 2, (c + 1) * (JB // CHUNKS) // 2):
            at = slice(8 * p, 8 * p + 8)
            left = jnp.concatenate([lhs[0, at], lhs[1, at], lhs[2, at, 0:64]], axis=1).astype(BF16)
            both = jnp.concatenate([held[2 * p], held[2 * p + 1]], axis=1)
            got = jnp.dot(left, both, preferred_element_type=F32)
            total[8 * p : 8 * p + 8, :] = jnp.where(upper, got[:, :TB], got[:, TB:])
    mine = pl.ds(pl.multiple_of(slab_ref[0] * 8, 8), 8)
    total[mine, :] = total[mine, :] - measured_ref[...]
    out_ref[...] = total[...].astype(BF16)


def project(base, slab, keys, weights, before, rest, measured, blocks):
    return pl.pallas_call(
        project_kernel,
        out_shape=jax.ShapeDtypeStruct((JB * NB, TB), BF16),
        in_specs=[smem(), smem()]
        + [vmem()] * 8
        + [pl.BlockSpec(memory_space=pl.ANY)],
        out_specs=vmem(),
        scratch_shapes=[
            pltpu.VMEM((JB, KS * 64, TB), BF16),
            pltpu.VMEM((SHARD_ROWS, 256), BF16),
            pltpu.VMEM((3, JB * NB, 128), F32),
            pltpu.VMEM((JB * NB, TB), F32),
            pltpu.SemaphoreType.DMA((CHUNKS,)),
        ],
        compiler_params=params(24),
        cost_estimate=cost(4.0),
        name="project",
    )(base, slab, keys, weights, before, *rest, measured, blocks)


def adjoint_kernel(
    own_ref, one_ref, two_ref, three_ref, weights_ref, blocks_ref, out_ref, held, resid, back, sems
):
    copies = start_blocks(blocks_ref, held, sems)
    back[2] = jnp.zeros((JB * NB, 128), F32)
    total = own_ref[...].astype(F32) + one_ref[...].astype(F32)
    total = total + two_ref[...].astype(F32) + three_ref[...].astype(F32)
    resid[...] = total.astype(BF16).astype(F32)
    upper = lax.broadcasted_iota(I32, (8, KS * 64), 0) < 4
    dims = (((1,), (1,)), ((), ()))
    for c in range(CHUNKS):
        copies[c].wait()
        for p in range(c * (JB // CHUNKS) // 2, (c + 1) * (JB // CHUNKS) // 2):
            left = resid[8 * p : 8 * p + 8, :].astype(BF16)
            a = lax.dot_general(left, held[2 * p], dims, preferred_element_type=F32)
            b = lax.dot_general(left, held[2 * p + 1], dims, preferred_element_type=F32)
            got = jnp.where(upper, a, b)
            at = slice(8 * p, 8 * p + 8)
            back[0, at, :] = got[:, 0:128]
            back[1, at, :] = got[:, 128:256]
            back[2, at, 0:64] = got[:, 256 : KS * 64]
    low = lower_half(JB)
    for m in range(2):
        for q in range(3):
            one = back[q, pl.ds(2 * m, JB, stride=4), :]
            two = back[q, pl.ds(2 * m + 1, JB, stride=4), :]
            even, odd = pair_halves(one, two, low)
            for k, part in ((2 * q, even), (2 * q + 1, odd)):
                if k < KS:
                    scaled = part * weights_ref[k * JB : (k + 1) * JB, :]
                    out_ref[k * JB : (k + 1) * JB, 128 * m : 128 * m + 128] = scaled.astype(BF16)


def adjoint(parts, weights, blocks):
    return pl.pallas_call(
        adjoint_kernel,
        out_shape=jax.ShapeDtypeStruct((SLOTS, 256), BF16),
        in_specs=[vmem()] * 5 + [pl.BlockSpec(memory_space=pl.ANY)],
        out_specs=vmem(),
        scratch_shapes=[
            pltpu.VMEM((JB, KS * 64, TB), BF16),
            pltpu.VMEM((JB * NB, TB), F32),
            pltpu.VMEM((3, JB * NB, 128), F32),
            pltpu.SemaphoreType.DMA((CHUNKS,)),
        ],
        compiler_params=params(24),
        cost_estimate=cost(4.0),
        name="adjoint",
    )(*parts, weights, blocks)


def rows_to_planes(rows, out_ref):
    low = lower_half(48)
    for m in range(2):
        for q in range(4):
            one = rows[96 * q : 96 * q + 48, 128 * m : 128 * m + 128]
            two = rows[96 * q + 48 : 96 * q + 96, 128 * m : 128 * m + 128]
            even, odd = pair_halves(one, two, low)
            out_ref[2 * m, q] = even
            out_ref[2 * m + 1, q] = odd


def edge_rows(planes_ref, place, z):
    for n in range(NB):
        for q in range(4):
            rows = planes_ref[n, q, pl.ds(z, 6, stride=8), :]
            place[n * 6 : n * 6 + 6, 128 * q : 128 * q + 128] = rows


def images_kernel(
    pos_ref,
    own_ref,
    plus_ref,
    minus_ref,
    *refs,
):
    others, (planes_ref, low_ref, high_ref, index_ref, rows) = refs[:-5], refs[-5:]
    sensor, last = pos_ref[0], pos_ref[1]
    keep_low = jnp.where(sensor > 0, 1.0, 0.0).astype(F32)
    keep_high = jnp.where(sensor < last, 1.0, 0.0).astype(F32)
    for h in range(8):
        block = slice(32 * h, 32 * h + 32)
        rows[48 * h : 48 * h + 8, :] = plus_ref[block, :].astype(F32)[24:32] * keep_low
        rows[48 * h + 8 : 48 * h + 40, :] = own_ref[block, :].astype(F32)
        rows[48 * h + 40 : 48 * h + 48, :] = minus_ref[block, :].astype(F32)[0:8] * keep_high
    rows_to_planes(rows, planes_ref)
    edge_rows(planes_ref, low_ref, 0)
    edge_rows(planes_ref, high_ref, 7)
    sources = [own_ref, plus_ref, minus_ref, *others[:-1]]
    for g in range(8):
        if g < 7:
            coded = sources[g][OWN:SHARD_ROWS, :].astype(F32)
        else:
            coded = others[-1][OWN - SPLIT : SHARD_ROWS - SPLIT, :].astype(F32)
        ids = (coded[0:2] * 16.0 + coded[2:4]).astype(I32)
        x = (ids >> 6) - 4 * sensor + 1
        row = (ids & 7) * 48 + x * 8 + ((ids >> 3) & 7)
        index_ref[g] = jnp.where((x >= 0) & (x < 6), row, -1)


def images(pos, shards):
    return pl.pallas_call(
        images_kernel,
        out_shape=[
            jax.ShapeDtypeStruct((NB, 4, 48, 128), F32),
            jax.ShapeDtypeStruct((24, 512), F32),
            jax.ShapeDtypeStruct((24, 512), F32),
            jax.ShapeDtypeStruct((8, 2, 256), I32),
        ],
        in_specs=[smem()] + [vmem()] * len(shards),
        out_specs=[vmem()] * 4,
        scratch_shapes=[pltpu.VMEM((384, 256), F32)],
        compiler_params=params(16),
        cost_estimate=cost(2.0),
        name="images_to_planes",
    )(pos, *shards)


def add_scattered(acc, index, contrib):
    first = lax.broadcasted_iota(I32, (384, 256), 0)
    second = lax.broadcasted_iota(I32, (384, SLOTS - 256), 0)
    hot = jnp.where(first == index[0:1, :], 1.0, 0.0).astype(BF16)
    more = jnp.where(second == index[1:2, 0 : SLOTS - 256], 1.0, 0.0).astype(BF16)
    acc = acc + jnp.dot(hot, contrib[0:256, :], preferred_element_type=F32)
    return acc + jnp.dot(more, contrib[256:SLOTS, :], preferred_element_type=F32)


def scatter_kernel(index_ref, *refs):
    contribs, out_ref = refs[:-1], refs[-1]
    acc = jnp.zeros((384, 256), F32)
    for i, contrib in enumerate(contribs):
        acc = add_scattered(acc, index_ref[i], contrib)
    out_ref[...] = acc


def scatter_first(index, contribs):
    return pl.pallas_call(
        scatter_kernel,
        out_shape=jax.ShapeDtypeStruct((384, 256), F32),
        in_specs=[vmem()] * (1 + len(contribs)),
        out_specs=vmem(),
        compiler_params=params(16),
        cost_estimate=cost(2.0),
        name="scatter_first",
    )(index, *contribs)


def gradient_kernel(
    index_ref,
    before_ref,
    three_ref,
    minus_ref,
    half_a_ref,
    half_b_ref,
    image_low_ref,
    image_high_ref,
    planes_ref,
    low_ref,
    high_ref,
    far,
    rows,
    edge,
):
    far[0 : SLOTS // 2, :] = half_a_ref[...]
    far[SLOTS // 2 : SLOTS, :] = half_b_ref[...]
    acc = before_ref[...]
    for i, contrib in enumerate((three_ref, minus_ref, far)):
        acc = add_scattered(acc, index_ref[5 + i], contrib)
    rows[...] = acc
    rows_to_planes(rows, planes_ref)
    edge[0:24, :] = image_low_ref[...]
    edge_rows(planes_ref, edge.at[pl.ds(24, 24)], 0)
    low_ref[...] = edge[...].astype(BF16)
    edge[0:24, :] = image_high_ref[...]
    edge_rows(planes_ref, edge.at[pl.ds(24, 24)], 7)
    high_ref[...] = edge[...].astype(BF16)


def gradient_planes(index, before, rest, image_low, image_high):
    return pl.pallas_call(
        gradient_kernel,
        out_shape=[
            jax.ShapeDtypeStruct((NB, 4, 48, 128), F32),
            jax.ShapeDtypeStruct((48, 512), BF16),
            jax.ShapeDtypeStruct((48, 512), BF16),
        ],
        in_specs=[vmem()] * 8,
        out_specs=[vmem()] * 3,
        scratch_shapes=[
            pltpu.VMEM((SLOTS, 256), BF16),
            pltpu.VMEM((384, 256), F32),
            pltpu.VMEM((48, 512), F32),
        ],
        compiler_params=params(16),
        cost_estimate=cost(2.0),
        name="gradient_planes",
    )(index, before, *rest, image_low, image_high)


def shifted_rows(rows, e):
    if e == 1:
        return rows
    y = lax.broadcasted_iota(I32, rows.shape, 1)
    if e == 0:
        return jnp.where(y == 0, 0.0, pltpu.roll(rows, 1, axis=1))
    return jnp.where(y == 511, 0.0, pltpu.roll(rows, 511, axis=1))


def conv_kernel(
    image_ref, grad_ref, low_ref, high_ref, matrix_ref, out_w_ref, out_ref, body, ends, done
):
    for kind, (ref, start) in enumerate(((low_ref, 0), (high_ref, 0), (low_ref, 24), (high_ref, 24))):
        rows = ref[...].astype(F32)[start : start + 24]
        for e in range(3):
            moved = shifted_rows(rows, e)
            for q in range(4):
                ends[q, pl.ds(kind + 4 * e, 24, stride=16), :] = moved[:, 128 * q : 128 * q + 128]
    for q in range(4):
        ends[q, pl.ds(12, 24, stride=16), :] = jnp.ones((24, 128), F32)
        for r in range(13, 16):
            ends[q, pl.ds(r, 24, stride=16), :] = jnp.zeros((24, 128), F32)
    for n in range(NB):
        for x in range(6):
            rows = jnp.concatenate(
                [
                    jnp.concatenate([ref[n, q, 8 * x : 8 * x + 8, :] for q in range(4)], axis=1)
                    for ref in (image_ref, grad_ref)
                ],
                axis=0,
            )
            for e in range(3):
                body[e, n * 6 + x] = shifted_rows(rows, e).astype(BF16)

    def one_x(x, carry):
        for n in range(NB):
            for half in range(2):
                cols = slice(256 * half, 256 * half + 256)
                tiles = [body[e, n * 6 + x + a, :, cols] for a in range(3) for e in range(3)]
                for a in range(3):
                    at = pl.multiple_of((n * 6 + x + a) * 16, 16)
                    pair = [ends[2 * half + q, pl.ds(at, 16), :] for q in range(2)]
                    tiles.append(jnp.concatenate(pair, axis=1).astype(BF16))
                stack = jnp.concatenate(tiles, axis=0)
                hidden = jnp.dot(matrix_ref[0], stack, preferred_element_type=F32)
                hidden = hidden + jnp.dot(matrix_ref[1], stack, preferred_element_type=F32)
                at = pl.multiple_of(8 * x + 8, 8)
                pair = [image_ref[n, 2 * half + q, pl.ds(at, 8), :] for q in range(2)]
                total = jnp.concatenate(pair, axis=1)
                for c in range(CHAN):
                    total = total + jnp.maximum(hidden[8 * c : 8 * c + 8], 0.0) * out_w_ref[c]
                for q in range(2):
                    part = total[:, 128 * q : 128 * q + 128]
                    done[2 * half + q, pl.ds(n, 8, stride=4), :] = part
        for z in range(8):
            for q in range(4):
                out_ref[x, z, :, 128 * q : 128 * q + 128] = done[q, 4 * z : 4 * z + 4, :]
        return carry

    lax.fori_loop(0, 4, one_x, 0)


def convolve(image, grad, low, high, matrix, out_w):
    return pl.pallas_call(
        conv_kernel,
        out_shape=jax.ShapeDtypeStruct((4, 8, NB, 512), F32),
        in_specs=[vmem()] * 5 + [smem()],
        out_specs=vmem(),
        scratch_shapes=[
            pltpu.VMEM((3, 24, 16, 512), BF16),
            pltpu.VMEM((4, 384, 128), F32),
            pltpu.VMEM((4, 32, 128), F32),
        ],
        compiler_params=params(32),
        cost_estimate=cost(5.0),
        name="convolutions",
    )(image, grad, low, high, matrix, out_w)


def tap_choice():
    choice = np.zeros((55, 8, TAPS), np.float32)
    for z in range(8):
        for a in range(3):
            for e in range(3):
                for i in range(2):
                    for plane in range(-1, 9):
                        b = plane - z + 1
                        if not 0 <= b <= 2:
                            continue
                        if 0 <= plane < 8:
                            column = (a * 3 + e) * 16 + i * 8 + plane
                        else:
                            column = 144 + a * 16 + i * 2 + (plane > 0) + 4 * e
                        choice[i * 27 + (a * 3 + b) * 3 + e, z, column] = 1.0
        choice[54, z, 144 + 12] = 1.0
    return choice


def conv_matrix(conv_in, conv_bias):
    table = jnp.concatenate([conv_in.reshape(CHAN, 54), conv_bias[:, None]], axis=1)
    high = lax.reduce_precision(table, 8, 7)
    parts = jnp.concatenate([high, table - high], axis=0).astype(BF16)
    choice = jnp.asarray(tap_choice().reshape(55, 8 * TAPS), BF16)
    spread = jnp.dot(parts, choice, preferred_element_type=F32).astype(BF16)
    return spread.reshape(2, CHAN * 8, TAPS)


def ring(distance, count):
    return [(i, (i + distance) % count) for i in range(count)]


def slab_perm(dy, dx, core):
    def index(y, x, c):
        return (y % 4 * 4 + x % 4) * 2 + c

    return [
        (index(y, x, c), index(y + dy, x + dx, c ^ core))
        for y in range(4)
        for x in range(4)
        for c in range(2)
    ]


def from_sensor(block, distance):
    return lax.ppermute(block, "sensor", ring(distance, 8))


def spread_near(block):
    return [from_sensor(block, d) for d in (1, -1, 2, -2)]


def spread_far(near, split):
    plus, minus = near[2], near[3]
    return [
        from_sensor(plus, 1),
        from_sensor(minus, -1),
        from_sensor(plus[:split], 2),
        from_sensor(minus[split:], -2),
    ]


def slab_sum_parts(partial):
    other = lax.ppermute(partial, "slab", slab_perm(0, 0, 1))
    total = partial.astype(F32) + other.astype(F32)
    total = total.astype(BF16)
    moved = [lax.ppermute(total, "slab", slab_perm(0, d, 0)) for d in (1, 3, 2)]
    row = total.astype(F32) + moved[0].astype(F32) + moved[1].astype(F32) + moved[2].astype(F32)
    row = row.astype(BF16)
    return [row] + [lax.ppermute(row, "slab", slab_perm(d, 0, 0)) for d in (1, 3, 2)]


def slot_weights(live_slots, exponents):
    slot_iota = lax.broadcasted_iota(I32, exponents.shape, 1)
    scaled = jnp.exp2(exponents.astype(F32))
    return jnp.where(slot_iota < live_slots[:, None], scaled, jnp.zeros_like(scaled))


def on_device(volume, measured, blocks, voxel_ids, counts, exponents, conv_in, conv_bias, conv_out):
    sensor = lax.axis_index("sensor").astype(I32)
    slab = lax.axis_index("slab").astype(I32)
    steps = jnp.array([0, -1, 1, -2, 2, -3, 3, 4], I32)
    base = ((sensor + steps) % 8) * OWN
    pos = jnp.stack([sensor, jnp.full_like(sensor, 7)])
    ids = voxel_ids.T.reshape(SLOTS)
    padded = jnp.pad(ids, (0, 512 - SLOTS), constant_values=4080).reshape(2, 256)
    id_rows = jnp.concatenate([padded >> 4, padded & 15, jnp.zeros((12, 256), I32)], axis=0)
    keys = (ids & ~255) | ((ids & 7) << 5) | ((ids >> 3) & 31)
    keys = keys.reshape(SLOTS, 1)
    weights = slot_weights(counts[:, 0], exponents).T.reshape(SLOTS, 1)
    stacked = blocks.reshape(JB, KS * 64, TB)

    shard = prep(volume, id_rows.astype(BF16))
    near = spread_near(shard)
    far = spread_far(near, SPLIT)
    before = gather_first(base, keys, weights, [shard, *near])
    partial = project(
        base, slab.reshape(1), keys, weights, before, far,
        measured.reshape(8, TB).astype(F32), stacked,
    )
    parts = slab_sum_parts(partial)
    matrix = conv_matrix(conv_in, conv_bias)
    image, image_low, image_high, index = images(
        pos, [shard, *near, far[0], far[1], far[3]]
    )
    contrib = adjoint(parts, weights, stacked)
    near_c = spread_near(contrib)
    far_c = spread_far(near_c, SLOTS // 2)
    sums = scatter_first(index, [contrib, *near_c])
    grad, low_out, high_out = gradient_planes(index, sums, far_c, image_low, image_high)
    forward = [(i, i + 1) for i in range(31)]
    backward = [(i + 1, i) for i in range(31)]
    low_in = lax.ppermute(high_out, "slab", forward)
    high_in = lax.ppermute(low_out, "slab", backward)
    return convolve(image, grad, low_in, high_in, matrix, conv_out)


def solution(mesh):
    in_specs = (
        P("sensor", "slab", None, None),
        P(("sensor", "slab"), None, None),
        P("sensor", "slab", None, None),
        P("sensor", "slab"),
        P("sensor", "slab"),
        P("sensor", "slab"),
        P(),
        P(),
        P(),
    )
    out_specs = P("sensor", "slab", None, None)
    return jax.shard_map(
        on_device, mesh=mesh, in_specs=in_specs, out_specs=out_specs, check_vma=False
    )
```

```python
import functools

import jax
import jax.numpy as jnp
import numpy as np
from jax import lax
from jax.experimental import pallas as pl
from jax.experimental.pallas import tpu as pltpu
from jax.sharding import PartitionSpec as P

F32 = jnp.float32
BF16 = jnp.bfloat16
I32 = jnp.int32

JB = 64
KS = 5
SLOTS = JB * KS
NB = 4
TB = 128
OWN = 256
SENT = SLOTS + 16
SENT_SPLIT = 176
CHAN = 32
TAPS = 192


def vmem():
    return pl.BlockSpec(memory_space=pltpu.VMEM)


def smem():
    return pl.BlockSpec(memory_space=pltpu.SMEM)


def params(mib):
    return pltpu.CompilerParams(vmem_limit_bytes=mib * 1024 * 1024)


def cost(us):
    return pl.CostEstimate(flops=0, bytes_accessed=int(us * 3.0e6), transcendentals=0)


def lower_half(rows):
    return lax.broadcasted_iota(I32, (rows, 128), 1) < 64


def swapped(tile):
    return pltpu.roll(tile, 64, axis=1)


def pair_halves(first, second, low):
    return jnp.where(low, first, swapped(second)), jnp.where(low, swapped(first), second)


def planes_to_rows(volume_refs, rows, out_ref):
    i = 0
    for volume_ref in volume_refs:
        for x in range(volume_ref.shape[0]):
            for z in range(8):
                image = volume_ref[x, z].astype(F32)
                for q in range(4):
                    rows[q, 4 * i : 4 * i + 4, :] = image[:, 128 * q : 128 * q + 128]
                i += 1
    low = lower_half(32)
    for m in range(2):
        for q in range(4):
            one = rows[q, pl.ds(2 * m, 32, stride=4), :]
            two = rows[q, pl.ds(2 * m + 1, 32, stride=4), :]
            even, odd = pair_halves(one, two, low)
            out_ref[64 * q : 64 * q + 32, 128 * m : 128 * m + 128] = even.astype(BF16)
            out_ref[64 * q + 32 : 64 * q + 64, 128 * m : 128 * m + 128] = odd.astype(BF16)


def add_gathered(acc, keys, weights, base, shard):
    lane = lax.broadcasted_iota(I32, (SLOTS, OWN), 1)
    hot = jnp.where(lane == keys - base, weights, 0.0).astype(BF16)
    return acc + jnp.dot(hot, shard, preferred_element_type=F32)


def gather_kernel(
    base_ref, keys_ref, weights_ref, own_ref, plus_ref, minus_ref, two_ref, back_ref,
    out_ref, own_rows, plus_rows, minus_rows, rows, shard,
):
    acc = jnp.zeros((SLOTS, 256), F32)
    keys, weights = keys_ref[...], weights_ref[...]
    shards = (own_rows, plus_rows, minus_rows, shard.at[0], shard.at[1])
    for i, ref in enumerate((own_ref, plus_ref, minus_ref, two_ref, back_ref)):
        planes_to_rows([ref], rows.at[i], shards[i])
        acc = add_gathered(acc, keys, weights, base_ref[i], shards[i][...])
    out_ref[...] = acc


def gather_first(base, keys, weights, shards):
    return pl.pallas_call(
        gather_kernel,
        out_shape=[jax.ShapeDtypeStruct((SLOTS, 256), F32)]
        + [jax.ShapeDtypeStruct((OWN, 256), BF16)] * 3,
        in_specs=[smem()] + [vmem()] * (2 + len(shards)),
        out_specs=[vmem()] * 4,
        scratch_shapes=[
            pltpu.VMEM((5, 4, 128, 128), F32),
            pltpu.VMEM((2, OWN, 256), BF16),
        ],
        compiler_params=params(16),
        cost_estimate=cost(1.5),
        name="gather_first",
    )(base, keys, weights, *shards)


CHUNKS = 8


def hold_kernel(blocks_ref, after_ref, held_ref, sems):
    step = JB // CHUNKS
    copies = [
        pltpu.make_async_copy(
            blocks_ref.at[pl.ds(c * step, step)], held_ref.at[pl.ds(c * step, step)], sems.at[c]
        )
        for c in range(CHUNKS)
    ]
    for copy in copies:
        copy.start()
    for copy in copies:
        copy.wait()


def hold(blocks, after):
    return pl.pallas_call(
        hold_kernel,
        out_shape=jax.ShapeDtypeStruct((JB, KS * 64, TB), BF16),
        in_specs=[pl.BlockSpec(memory_space=pl.ANY), pl.BlockSpec(memory_space=pl.ANY)],
        out_specs=vmem(),
        scratch_shapes=[pltpu.SemaphoreType.DMA((CHUNKS,))],
        compiler_params=params(46),
        cost_estimate=cost(2.5),
        name="hold_blocks",
    )(blocks, after)


def project_kernel(
    base_ref,
    slab_ref,
    keys_ref,
    weights_ref,
    before_ref,
    three_ref,
    minus_ref,
    half_a_ref,
    half_b_ref,
    measured_ref,
    held,
    out_ref,
    rows,
    shard,
    lhs,
    total,
):
    acc = before_ref[...]
    keys, weights = keys_ref[...], weights_ref[...]
    for i, refs in enumerate(((three_ref,), (minus_ref,), (half_a_ref, half_b_ref))):
        planes_to_rows(refs, rows.at[i], shard.at[i])
        acc = add_gathered(acc, keys, weights, base_ref[5 + i], shard[i])
    low = lower_half(JB)
    for m in range(2):
        cols = slice(128 * m, 128 * m + 128)
        for q in range(3):
            one = acc[2 * q * JB : (2 * q + 1) * JB, cols]
            if q < 2:
                two = acc[(2 * q + 1) * JB : (2 * q + 2) * JB, cols]
                even, odd = pair_halves(one, two, low)
            else:
                even, odd = one, swapped(one)
            lhs[q, pl.ds(2 * m, JB, stride=4), :] = even
            lhs[q, pl.ds(2 * m + 1, JB, stride=4), :] = odd
    upper = lax.broadcasted_iota(I32, (8, TB), 0) < 4
    for p in range(JB // 2):
        at = slice(8 * p, 8 * p + 8)
        left = jnp.concatenate([lhs[0, at], lhs[1, at], lhs[2, at, 0:64]], axis=1).astype(BF16)
        both = jnp.concatenate([held[2 * p], held[2 * p + 1]], axis=1)
        got = jnp.dot(left, both, preferred_element_type=F32)
        total[8 * p : 8 * p + 8, :] = jnp.where(upper, got[:, :TB], got[:, TB:])
    mine = pl.ds(pl.multiple_of(slab_ref[0] * 8, 8), 8)
    total[mine, :] = total[mine, :] - measured_ref[...]
    out_ref[...] = total[...].astype(BF16)


def project(base, slab, keys, weights, before, rest, measured, held):
    return pl.pallas_call(
        project_kernel,
        out_shape=jax.ShapeDtypeStruct((JB * NB, TB), BF16),
        in_specs=[smem(), smem()] + [vmem()] * 9,
        out_specs=vmem(),
        scratch_shapes=[
            pltpu.VMEM((3, 4, 128, 128), F32),
            pltpu.VMEM((3, OWN, 256), BF16),
            pltpu.VMEM((3, JB * NB, 128), F32),
            pltpu.VMEM((JB * NB, TB), F32),
        ],
        compiler_params=params(16),
        cost_estimate=cost(4.0),
        name="project",
    )(base, slab, keys, weights, before, *rest, measured, held)


def adjoint_kernel(
    own_ref, one_ref, two_ref, three_ref, weights_ref, ids_ref, held, out_ref, resid, back
):
    back[2] = jnp.zeros((JB * NB, 128), F32)
    total = own_ref[...].astype(F32) + one_ref[...].astype(F32)
    total = total + two_ref[...].astype(F32) + three_ref[...].astype(F32)
    resid[...] = total.astype(BF16).astype(F32)
    upper = lax.broadcasted_iota(I32, (8, KS * 64), 0) < 4
    dims = (((1,), (1,)), ((), ()))
    for p in range(JB // 2):
        left = resid[8 * p : 8 * p + 8, :].astype(BF16)
        a = lax.dot_general(left, held[2 * p], dims, preferred_element_type=F32)
        b = lax.dot_general(left, held[2 * p + 1], dims, preferred_element_type=F32)
        got = jnp.where(upper, a, b)
        at = slice(8 * p, 8 * p + 8)
        back[0, at, :] = got[:, 0:128]
        back[1, at, :] = got[:, 128:256]
        back[2, at, 0:64] = got[:, 256 : KS * 64]
    low = lower_half(JB)
    for m in range(2):
        for q in range(3):
            one = back[q, pl.ds(2 * m, JB, stride=4), :]
            two = back[q, pl.ds(2 * m + 1, JB, stride=4), :]
            even, odd = pair_halves(one, two, low)
            for k, part in ((2 * q, even), (2 * q + 1, odd)):
                if k < KS:
                    scaled = part * weights_ref[k * JB : (k + 1) * JB, :]
                    out_ref[k * JB : (k + 1) * JB, 128 * m : 128 * m + 128] = scaled.astype(BF16)
    out_ref[SLOTS:SENT, :] = ids_ref[...]


def adjoint(parts, weights, id_rows, held):
    return pl.pallas_call(
        adjoint_kernel,
        out_shape=jax.ShapeDtypeStruct((SENT, 256), BF16),
        in_specs=[vmem()] * 7,
        out_specs=vmem(),
        scratch_shapes=[
            pltpu.VMEM((JB * NB, TB), F32),
            pltpu.VMEM((3, JB * NB, 128), F32),
        ],
        compiler_params=params(16),
        cost_estimate=cost(3.0),
        name="adjoint",
    )(*parts, weights, id_rows, held)


def rows_to_planes(rows, out_ref):
    low = lower_half(48)
    for m in range(2):
        for q in range(4):
            one = rows[96 * q : 96 * q + 48, 128 * m : 128 * m + 128]
            two = rows[96 * q + 48 : 96 * q + 96, 128 * m : 128 * m + 128]
            even, odd = pair_halves(one, two, low)
            out_ref[2 * m, q] = even
            out_ref[2 * m + 1, q] = odd


def edge_rows(planes_ref, place, z):
    for n in range(NB):
        for q in range(4):
            rows = planes_ref[n, q, pl.ds(z, 6, stride=8), :]
            place[n * 6 : n * 6 + 6, 128 * q : 128 * q + 128] = rows


def images_kernel(
    pos_ref, own_ref, plus_ref, minus_ref, planes_ref, low_ref, high_ref, rows
):
    sensor, last = pos_ref[0], pos_ref[1]
    keep_low = jnp.where(sensor > 0, 1.0, 0.0).astype(F32)
    keep_high = jnp.where(sensor < last, 1.0, 0.0).astype(F32)
    for h in range(8):
        block = slice(32 * h, 32 * h + 32)
        rows[48 * h : 48 * h + 8, :] = plus_ref[block, :].astype(F32)[24:32] * keep_low
        rows[48 * h + 8 : 48 * h + 40, :] = own_ref[block, :].astype(F32)
        rows[48 * h + 40 : 48 * h + 48, :] = minus_ref[block, :].astype(F32)[0:8] * keep_high
    rows_to_planes(rows, planes_ref)
    edge_rows(planes_ref, low_ref, 0)
    edge_rows(planes_ref, high_ref, 7)


def images(pos, shards):
    return pl.pallas_call(
        images_kernel,
        out_shape=[
            jax.ShapeDtypeStruct((NB, 4, 48, 128), F32),
            jax.ShapeDtypeStruct((24, 512), F32),
            jax.ShapeDtypeStruct((24, 512), F32),
        ],
        in_specs=[smem()] + [vmem()] * len(shards),
        out_specs=[vmem()] * 3,
        scratch_shapes=[pltpu.VMEM((384, 256), F32)],
        compiler_params=params(16),
        cost_estimate=cost(0.7),
        name="images_to_planes",
    )(pos, *shards)


def add_scattered(acc, sensor, contrib):
    coded = contrib[SLOTS:SENT, :].astype(F32)
    ids = (coded[0:2] * 16.0 + coded[2:4]).astype(I32)
    x = (ids >> 6) - 4 * sensor + 1
    index = (ids & 7) * 48 + x * 8 + ((ids >> 3) & 7)
    index = jnp.where((x >= 0) & (x < 6), index, -1)
    first = lax.broadcasted_iota(I32, (384, 256), 0)
    second = lax.broadcasted_iota(I32, (384, SLOTS - 256), 0)
    hot = jnp.where(first == index[0:1, :], 1.0, 0.0).astype(BF16)
    more = jnp.where(second == index[1:2, 0 : SLOTS - 256], 1.0, 0.0).astype(BF16)
    acc = acc + jnp.dot(hot, contrib[0:256, :], preferred_element_type=F32)
    return acc + jnp.dot(more, contrib[256:SLOTS, :], preferred_element_type=F32)


def scatter_kernel(pos_ref, *refs):
    contribs, out_ref = refs[:-1], refs[-1]
    acc = jnp.zeros((384, 256), F32)
    for contrib in contribs:
        acc = add_scattered(acc, pos_ref[0], contrib)
    out_ref[...] = acc


def scatter_first(pos, contribs):
    return pl.pallas_call(
        scatter_kernel,
        out_shape=jax.ShapeDtypeStruct((384, 256), F32),
        in_specs=[smem()] + [vmem()] * len(contribs),
        out_specs=vmem(),
        compiler_params=params(16),
        cost_estimate=cost(0.7),
        name="scatter_first",
    )(pos, *contribs)


def gradient_kernel(
    pos_ref,
    before_ref,
    three_ref,
    minus_ref,
    half_a_ref,
    half_b_ref,
    image_low_ref,
    image_high_ref,
    planes_ref,
    inner_ref,
    outer_ref,
    far,
    rows,
    low,
    high,
):
    far[0:SENT_SPLIT, :] = half_a_ref[...]
    far[SENT_SPLIT:SENT, :] = half_b_ref[...]
    acc = before_ref[...]
    for contrib in (three_ref, minus_ref, far):
        acc = add_scattered(acc, pos_ref[0], contrib)
    rows[...] = acc
    rows_to_planes(rows, planes_ref)
    low[0:24, :] = image_low_ref[...]
    high[0:24, :] = image_high_ref[...]
    edge_rows(planes_ref, low.at[pl.ds(24, 24)], 0)
    edge_rows(planes_ref, high.at[pl.ds(24, 24)], 7)
    first_core = pos_ref[2] == 0
    inner_ref[...] = jnp.where(first_core, high[...], low[...]).astype(BF16)
    outer_ref[...] = jnp.where(first_core, low[...], high[...]).astype(BF16)


def gradient_planes(pos, before, rest, image_low, image_high):
    return pl.pallas_call(
        gradient_kernel,
        out_shape=[
            jax.ShapeDtypeStruct((NB, 4, 48, 128), F32),
            jax.ShapeDtypeStruct((48, 512), BF16),
            jax.ShapeDtypeStruct((48, 512), BF16),
        ],
        in_specs=[smem()] + [vmem()] * 7,
        out_specs=[vmem()] * 3,
        scratch_shapes=[
            pltpu.VMEM((SENT, 256), BF16),
            pltpu.VMEM((384, 256), F32),
            pltpu.VMEM((48, 512), F32),
            pltpu.VMEM((48, 512), F32),
        ],
        compiler_params=params(16),
        cost_estimate=cost(1.0),
        name="gradient_planes",
    )(pos, before, *rest, image_low, image_high)


def shifted_rows(rows, e):
    if e == 1:
        return rows
    y = lax.broadcasted_iota(I32, rows.shape, 1)
    if e == 0:
        return jnp.where(y == 0, 0.0, pltpu.roll(rows, 1, axis=1))
    return jnp.where(y == 511, 0.0, pltpu.roll(rows, 511, axis=1))


def conv_kernel(
    pos_ref, image_ref, grad_ref, inner_ref, outer_ref, matrix_ref, out_w_ref, out_ref,
    body, ends, done,
):
    first_core = pos_ref[2] == 0
    inner, outer = inner_ref[...].astype(F32), outer_ref[...].astype(F32)
    below, above = jnp.where(first_core, outer, inner), jnp.where(first_core, inner, outer)
    for kind, (edge, start) in enumerate(((below, 0), (above, 0), (below, 24), (above, 24))):
        rows = edge[start : start + 24]
        for e in range(3):
            moved = shifted_rows(rows, e)
            for q in range(4):
                ends[q, pl.ds(kind + 4 * e, 24, stride=16), :] = moved[:, 128 * q : 128 * q + 128]
    for q in range(4):
        ends[q, pl.ds(12, 24, stride=16), :] = jnp.ones((24, 128), F32)
        for r in range(13, 16):
            ends[q, pl.ds(r, 24, stride=16), :] = jnp.zeros((24, 128), F32)
    for n in range(NB):
        for x in range(6):
            rows = jnp.concatenate(
                [
                    jnp.concatenate([ref[n, q, 8 * x : 8 * x + 8, :] for q in range(4)], axis=1)
                    for ref in (image_ref, grad_ref)
                ],
                axis=0,
            )
            for e in range(3):
                body[e, n * 6 + x] = shifted_rows(rows, e).astype(BF16)

    def one_x(x, carry):
        for n in range(NB):
            for half in range(2):
                cols = slice(256 * half, 256 * half + 256)
                tiles = [body[e, n * 6 + x + a, :, cols] for a in range(3) for e in range(3)]
                for a in range(3):
                    at = pl.multiple_of((n * 6 + x + a) * 16, 16)
                    pair = [ends[2 * half + q, pl.ds(at, 16), :] for q in range(2)]
                    tiles.append(jnp.concatenate(pair, axis=1).astype(BF16))
                stack = jnp.concatenate(tiles, axis=0)
                hidden = jnp.dot(matrix_ref[0], stack, preferred_element_type=F32)
                hidden = hidden + jnp.dot(matrix_ref[1], stack, preferred_element_type=F32)
                at = pl.multiple_of(8 * x + 8, 8)
                pair = [image_ref[n, 2 * half + q, pl.ds(at, 8), :] for q in range(2)]
                total = jnp.concatenate(pair, axis=1)
                for c in range(CHAN):
                    total = total + jnp.maximum(hidden[8 * c : 8 * c + 8], 0.0) * out_w_ref[c]
                for q in range(2):
                    part = total[:, 128 * q : 128 * q + 128]
                    done[2 * half + q, pl.ds(n, 8, stride=4), :] = part
        for z in range(8):
            for q in range(4):
                out_ref[x, z, :, 128 * q : 128 * q + 128] = done[q, 4 * z : 4 * z + 4, :]
        return carry

    lax.fori_loop(0, 4, one_x, 0)


def convolve(pos, image, grad, inner, outer, matrix, out_w):
    return pl.pallas_call(
        conv_kernel,
        out_shape=jax.ShapeDtypeStruct((4, 8, NB, 512), F32),
        in_specs=[smem()] + [vmem()] * 5 + [smem()],
        out_specs=vmem(),
        scratch_shapes=[
            pltpu.VMEM((3, 24, 16, 512), BF16),
            pltpu.VMEM((4, 384, 128), F32),
            pltpu.VMEM((4, 32, 128), F32),
        ],
        compiler_params=params(32),
        cost_estimate=cost(5.0),
        name="convolutions",
    )(pos, image, grad, inner, outer, matrix, out_w)


def tap_choice():
    choice = np.zeros((55, 8, TAPS), np.float32)
    for z in range(8):
        for a in range(3):
            for e in range(3):
                for i in range(2):
                    for plane in range(-1, 9):
                        b = plane - z + 1
                        if not 0 <= b <= 2:
                            continue
                        if 0 <= plane < 8:
                            column = (a * 3 + e) * 16 + i * 8 + plane
                        else:
                            column = 144 + a * 16 + i * 2 + (plane > 0) + 4 * e
                        choice[i * 27 + (a * 3 + b) * 3 + e, z, column] = 1.0
        choice[54, z, 144 + 12] = 1.0
    return choice


def conv_matrix(conv_in, conv_bias):
    table = jnp.concatenate([conv_in.reshape(CHAN, 54), conv_bias[:, None]], axis=1)
    high = lax.reduce_precision(table, 8, 7)
    parts = jnp.concatenate([high, table - high], axis=0).astype(BF16)
    choice = jnp.asarray(tap_choice().reshape(55, 8 * TAPS), BF16)
    spread = jnp.dot(parts, choice, preferred_element_type=F32).astype(BF16)
    return spread.reshape(2, CHAN * 8, TAPS)


def ring(distance, count):
    return [(i, (i + distance) % count) for i in range(count)]


def slab_perm(dy, dx, core):
    def index(y, x, c):
        return (y % 4 * 4 + x % 4) * 2 + c

    return [
        (index(y, x, c), index(y + dy, x + dx, c ^ core))
        for y in range(4)
        for x in range(4)
        for c in range(2)
    ]


def from_sensor(block, distance):
    return lax.ppermute(block, "sensor", ring(distance, 8))


def spread_far(plus, minus, split):
    return [
        from_sensor(plus, 1),
        from_sensor(minus, -1),
        from_sensor(plus[:split], 2),
        from_sensor(minus[split:], -2),
    ]


def chip_sum(partial):
    other = lax.ppermute(partial, "slab", slab_perm(0, 0, 1))
    total = partial.astype(F32) + other.astype(F32)
    return total.astype(BF16)


def slab_sum_parts(total):
    moved = [lax.ppermute(total, "slab", slab_perm(0, d, 0)) for d in (1, 3, 2)]
    row = total.astype(F32) + moved[0].astype(F32) + moved[1].astype(F32) + moved[2].astype(F32)
    row = row.astype(BF16)
    return [row] + [lax.ppermute(row, "slab", slab_perm(d, 0, 0)) for d in (1, 3, 2)]


def slot_weights(live_slots, exponents):
    slot_iota = lax.broadcasted_iota(I32, exponents.shape, 1)
    scaled = jnp.exp2(exponents.astype(F32))
    return jnp.where(slot_iota < live_slots[:, None], scaled, jnp.zeros_like(scaled))


def on_device(volume, measured, blocks, voxel_ids, counts, exponents, conv_in, conv_bias, conv_out):
    sensor = lax.axis_index("sensor").astype(I32)
    slab = lax.axis_index("slab").astype(I32)
    steps = jnp.array([0, -1, 1, -2, 2, -3, 3, 4], I32)
    base = ((sensor + steps) % 8) * OWN
    pos = jnp.stack([sensor, jnp.full_like(sensor, 7), slab % 2])
    ids = voxel_ids.T.reshape(SLOTS)
    padded = jnp.pad(ids, (0, 512 - SLOTS), constant_values=4080).reshape(2, 256)
    id_rows = jnp.concatenate([padded >> 4, padded & 15, jnp.zeros((12, 256), I32)], axis=0)
    keys = (ids & ~255) | ((ids & 7) << 5) | ((ids >> 3) & 31)
    keys = keys.reshape(SLOTS, 1)
    weights = slot_weights(counts[:, 0], exponents).T.reshape(SLOTS, 1)
    stacked = blocks.reshape(JB, KS * 64, TB)

    plus, minus = from_sensor(volume, 1), from_sensor(volume, -1)
    two, back = from_sensor(volume, 2), from_sensor(volume, -2)
    far = spread_far(two, back, 2)
    held = hold(stacked, two)
    before, *near = gather_first(base, keys, weights, [volume, plus, minus, two, back])
    partial = project(
        base, slab.reshape(1), keys, weights, before, far,
        measured.reshape(8, TB).astype(F32), held,
    )
    chip = chip_sum(partial)
    held = hold(stacked, chip)
    parts = slab_sum_parts(chip)
    matrix = conv_matrix(conv_in, conv_bias)
    image, image_low, image_high = images(pos, near)
    contrib = adjoint(parts, weights, id_rows.astype(BF16), held)
    two_c, back_c = from_sensor(contrib, 2), from_sensor(contrib, -2)
    near_c = [contrib, from_sensor(contrib, 1), from_sensor(contrib, -1)]
    far_c = spread_far(two_c, back_c, SENT_SPLIT)
    sums = scatter_first(pos, [*near_c, two_c, back_c])
    grad, inner, outer = gradient_planes(pos, sums, far_c, image_low, image_high)
    inner = lax.ppermute(inner, "slab", slab_perm(0, 0, 1))
    pairs = [(2 * i + 1, 2 * i + 2) for i in range(15)]
    outer = lax.ppermute(outer, "slab", pairs + [(b, a) for a, b in pairs])
    return convolve(pos, image, grad, inner, outer, matrix, conv_out)


def solution(mesh):
    in_specs = (
        P("sensor", "slab", None, None),
        P(("sensor", "slab"), None, None),
        P("sensor", "slab", None, None),
        P("sensor", "slab"),
        P("sensor", "slab"),
        P("sensor", "slab"),
        P(),
        P(),
        P(),
    )
    out_specs = P("sensor", "slab", None, None)
    return jax.shard_map(
        on_device, mesh=mesh, in_specs=in_specs, out_specs=out_specs, check_vma=False
    )
```

```python
import functools

import jax
import jax.numpy as jnp
import numpy as np
from jax import lax
from jax.experimental import pallas as pl
from jax.experimental.pallas import tpu as pltpu
from jax.sharding import PartitionSpec as P

F32 = jnp.float32
BF16 = jnp.bfloat16
I32 = jnp.int32

JB = 64
KS = 5
SLOTS = JB * KS
NB = 4
TB = 128
OWN = 256
CAP = 80
PACKED = CAP + 16
SENT = SLOTS + 16
SENT_SPLIT = 176
CHAN = 32
TAPS = 192


def owner_base(step):
    return lax.rem(lax.axis_index("sensor") + (step + 8), 8) * OWN


STEPS = (0, -1, 1, -2, 2, -3, 3, 4)


def vmem():
    return pl.BlockSpec(memory_space=pltpu.VMEM)


def smem():
    return pl.BlockSpec(memory_space=pltpu.SMEM)


def params(mib):
    return pltpu.CompilerParams(vmem_limit_bytes=mib * 1024 * 1024)


def cost(us):
    return pl.CostEstimate(flops=0, bytes_accessed=int(us * 3.0e6), transcendentals=0)


def lower_half(rows):
    return lax.broadcasted_iota(I32, (rows, 128), 1) < 64


def swapped(tile):
    return pltpu.roll(tile, 64, axis=1)


def pair_halves(first, second, low):
    return jnp.where(low, first, swapped(second)), jnp.where(low, swapped(first), second)


def planes_to_rows(volume_refs, rows, out_ref):
    i = 0
    for volume_ref in volume_refs:
        for x in range(volume_ref.shape[0]):
            for z in range(8):
                image = volume_ref[x, z].astype(F32)
                for q in range(4):
                    rows[q, 4 * i : 4 * i + 4, :] = image[:, 128 * q : 128 * q + 128]
                i += 1
    low = lower_half(32)
    for m in range(2):
        for q in range(4):
            one = rows[q, pl.ds(2 * m, 32, stride=4), :]
            two = rows[q, pl.ds(2 * m + 1, 32, stride=4), :]
            even, odd = pair_halves(one, two, low)
            out_ref[64 * q : 64 * q + 32, 128 * m : 128 * m + 128] = even.astype(BF16)
            out_ref[64 * q + 32 : 64 * q + 64, 128 * m : 128 * m + 128] = odd.astype(BF16)


def add_gathered(acc, keys, weights, base, shard):
    lane = lax.broadcasted_iota(I32, (SLOTS, OWN), 1)
    hot = jnp.where(lane == keys - base, weights, 0.0).astype(BF16)
    return acc + jnp.dot(hot, shard, preferred_element_type=F32)


def gather_kernel(
    keys_ref, weights_ref, own_ref, plus_ref, minus_ref, two_ref, back_ref,
    out_ref, own_rows, plus_rows, minus_rows, rows, shard,
):
    acc = jnp.zeros((SLOTS, 256), F32)
    keys, weights = keys_ref[...], weights_ref[...]
    shards = (own_rows, plus_rows, minus_rows, shard.at[0], shard.at[1])
    for i, ref in enumerate((own_ref, plus_ref, minus_ref, two_ref, back_ref)):
        planes_to_rows([ref], rows.at[i], shards[i])
        acc = add_gathered(acc, keys, weights, owner_base(STEPS[i]), shards[i][...])
    out_ref[...] = acc


def gather_first(keys, weights, shards):
    return pl.pallas_call(
        gather_kernel,
        out_shape=[jax.ShapeDtypeStruct((SLOTS, 256), F32)]
        + [jax.ShapeDtypeStruct((OWN, 256), BF16)] * 3,
        in_specs=[vmem()] * (2 + len(shards)),
        out_specs=[vmem()] * 4,
        scratch_shapes=[
            pltpu.VMEM((5, 4, 128, 128), F32),
            pltpu.VMEM((2, OWN, 256), BF16),
        ],
        compiler_params=params(16),
        cost_estimate=cost(1.5),
        name="gather_first",
    )(keys, weights, *shards)


CHUNKS = 8


def hold_kernel(start, blocks_ref, after_ref, held_ref, sems):
    step = held_ref.shape[0] // CHUNKS
    copies = [
        pltpu.make_async_copy(
            blocks_ref.at[pl.ds(start + c * step, step)],
            held_ref.at[pl.ds(c * step, step)],
            sems.at[c],
        )
        for c in range(CHUNKS)
    ]
    for copy in copies:
        copy.start()
    for copy in copies:
        copy.wait()


def hold(blocks, after, start=0, count=JB):
    return pl.pallas_call(
        functools.partial(hold_kernel, start),
        out_shape=jax.ShapeDtypeStruct((count, KS * 64, TB), BF16),
        in_specs=[pl.BlockSpec(memory_space=pl.ANY), pl.BlockSpec(memory_space=pl.ANY)],
        out_specs=vmem(),
        scratch_shapes=[pltpu.SemaphoreType.DMA((CHUNKS,))],
        compiler_params=params(46),
        cost_estimate=cost(2.5 * count / JB),
        name="hold_blocks",
    )(blocks, after)


def project_kernel(
    keys_ref,
    weights_ref,
    before_ref,
    three_ref,
    minus_ref,
    half_a_ref,
    half_b_ref,
    measured_ref,
    held,
    out_ref,
    rows,
    shard,
    lhs,
    total,
):
    acc = before_ref[...]
    keys, weights = keys_ref[...], weights_ref[...]
    for i, refs in enumerate(((three_ref,), (minus_ref,), (half_a_ref, half_b_ref))):
        planes_to_rows(refs, rows.at[i], shard.at[i])
        acc = add_gathered(acc, keys, weights, owner_base(STEPS[5 + i]), shard[i])
    low = lower_half(JB)
    for m in range(2):
        cols = slice(128 * m, 128 * m + 128)
        for q in range(3):
            one = acc[2 * q * JB : (2 * q + 1) * JB, cols]
            if q < 2:
                two = acc[(2 * q + 1) * JB : (2 * q + 2) * JB, cols]
                even, odd = pair_halves(one, two, low)
            else:
                even, odd = one, swapped(one)
            lhs[q, pl.ds(2 * m, JB, stride=4), :] = even
            lhs[q, pl.ds(2 * m + 1, JB, stride=4), :] = odd
    upper = lax.broadcasted_iota(I32, (8, TB), 0) < 4
    for p in range(JB // 2):
        at = slice(8 * p, 8 * p + 8)
        left = jnp.concatenate([lhs[0, at], lhs[1, at], lhs[2, at, 0:64]], axis=1).astype(BF16)
        both = jnp.concatenate([held[2 * p], held[2 * p + 1]], axis=1)
        got = jnp.dot(left, both, preferred_element_type=F32)
        total[8 * p : 8 * p + 8, :] = jnp.where(upper, got[:, :TB], got[:, TB:])
    mine = pl.ds(pl.multiple_of(lax.axis_index("slab") * 8, 8), 8)
    own = jnp.concatenate([measured_ref[0].astype(F32), measured_ref[1].astype(F32)], axis=0)
    total[mine, :] = total[mine, :] - own
    out_ref[...] = total[...].astype(BF16)


def project(keys, weights, before, rest, measured, held):
    return pl.pallas_call(
        project_kernel,
        out_shape=jax.ShapeDtypeStruct((JB * NB, TB), BF16),
        in_specs=[vmem()] * 9,
        out_specs=vmem(),
        scratch_shapes=[
            pltpu.VMEM((3, 4, 128, 128), F32),
            pltpu.VMEM((3, OWN, 256), BF16),
            pltpu.VMEM((3, JB * NB, 128), F32),
            pltpu.VMEM((JB * NB, TB), F32),
        ],
        compiler_params=params(16),
        cost_estimate=cost(4.0),
        name="project",
    )(keys, weights, before, *rest, measured, held)


def plan_kernel(ids_ref, weights_ref, choice_ref, places_ref):
    sensor = lax.axis_index("sensor")
    ids = jnp.broadcast_to(ids_ref[...], (8, SLOTS))
    live = jnp.broadcast_to(weights_ref[...], (8, SLOTS)) > 0.0
    step = lax.broadcasted_iota(I32, (8, SLOTS), 0)
    owner = lax.rem(sensor + step, 8)
    x = (ids >> 6) - 4 * owner + 1
    needed = live & (x >= 0) & (x < 6)
    place = (ids & 7) * 48 + x * 8 + ((ids >> 3) & 7)
    flags = jnp.where(needed, 1.0, 0.0)
    row = lax.broadcasted_iota(I32, (SLOTS, SLOTS), 0)
    column = lax.broadcasted_iota(I32, (SLOTS, SLOTS), 1)
    before = jnp.where(row < column, 1.0, 0.0).astype(BF16)
    rank = jnp.dot(flags.astype(BF16), before, preferred_element_type=F32)
    high = (place >> 4).astype(F32)
    low = (place & 15).astype(F32)
    most = jnp.max(jnp.sum(flags, axis=1, keepdims=True), axis=0, keepdims=True)
    over = jnp.where(most > CAP, 1.0, 0.0)
    want = lax.broadcasted_iota(I32, (CAP, SLOTS), 0).astype(F32)
    fill = jnp.zeros((4, SLOTS), F32)
    for d in range(8):
        at = slice(d, d + 1)
        rank_d = jnp.where(flags[at] > 0.0, rank[at], -1.0)
        hot = jnp.where(want == rank_d, 1.0, 0.0).astype(BF16)
        choice_ref[d * CAP : (d + 1) * CAP, :] = hot
        values = jnp.concatenate([high[at], low[at], flags[at], flags[at], fill], axis=0)
        coded = lax.dot_general(
            values.astype(BF16), hot, (((1,), (1,)), ((), ())), preferred_element_type=F32
        )
        coded = jnp.concatenate([coded, jnp.zeros((8, CAP), F32) + over], axis=0)
        wide = jnp.concatenate([coded, jnp.zeros((16, 128 - CAP), F32)], axis=1)
        wide = jnp.concatenate([wide, jnp.zeros((16, 128), F32)], axis=1)
        places_ref[d] = wide.astype(BF16)


def plan(ids, weights):
    return pl.pallas_call(
        plan_kernel,
        out_shape=[
            jax.ShapeDtypeStruct((8 * CAP, SLOTS), BF16),
            jax.ShapeDtypeStruct((8, 16, 256), BF16),
        ],
        in_specs=[vmem()] * 2,
        out_specs=[vmem()] * 2,
        compiler_params=params(16),
        cost_estimate=cost(1.5),
        name="plan_sends",
    )(ids, weights)


def adjoint_kernel(
    own_ref, one_ref, two_ref, three_ref, weights_ref, ids_ref, choice_ref, places_ref, held,
    out_ref, *refs,
):
    packed_refs, (resid, back) = refs[:8], refs[8:]
    back[2] = jnp.zeros((JB * NB, 128), F32)
    total = own_ref[...].astype(F32) + one_ref[...].astype(F32)
    total = total + two_ref[...].astype(F32) + three_ref[...].astype(F32)
    resid[...] = total.astype(BF16).astype(F32)
    upper = lax.broadcasted_iota(I32, (8, KS * 64), 0) < 4
    dims = (((1,), (1,)), ((), ()))
    for p in range(JB // 2):
        left = resid[8 * p : 8 * p + 8, :].astype(BF16)
        a = lax.dot_general(left, held[2 * p], dims, preferred_element_type=F32)
        b = lax.dot_general(left, held[2 * p + 1], dims, preferred_element_type=F32)
        got = jnp.where(upper, a, b)
        at = slice(8 * p, 8 * p + 8)
        back[0, at, :] = got[:, 0:128]
        back[1, at, :] = got[:, 128:256]
        back[2, at, 0:64] = got[:, 256 : KS * 64]
    low = lower_half(JB)
    for m in range(2):
        for q in range(3):
            one = back[q, pl.ds(2 * m, JB, stride=4), :]
            two = back[q, pl.ds(2 * m + 1, JB, stride=4), :]
            even, odd = pair_halves(one, two, low)
            for k, part in ((2 * q, even), (2 * q + 1, odd)):
                if k < KS:
                    scaled = part * weights_ref[k * JB : (k + 1) * JB, :]
                    out_ref[k * JB : (k + 1) * JB, 128 * m : 128 * m + 128] = scaled.astype(BF16)
    out_ref[SLOTS:SENT, :] = ids_ref[...]
    rows = out_ref[0:SLOTS, :]
    packed = jnp.dot(choice_ref[...], rows, preferred_element_type=F32).astype(BF16)
    for d, packed_ref in enumerate(packed_refs):
        packed_ref[0:CAP, :] = packed[d * CAP : (d + 1) * CAP]
        packed_ref[CAP:PACKED, :] = places_ref[d]


def adjoint(parts, weights, id_rows, choice, places, held):
    return pl.pallas_call(
        adjoint_kernel,
        out_shape=[jax.ShapeDtypeStruct((SENT, 256), BF16)]
        + [jax.ShapeDtypeStruct((PACKED, 256), BF16)] * 8,
        in_specs=[vmem()] * 9,
        out_specs=[vmem()] * 9,
        scratch_shapes=[
            pltpu.VMEM((JB * NB, TB), F32),
            pltpu.VMEM((3, JB * NB, 128), F32),
        ],
        compiler_params=params(16),
        cost_estimate=cost(3.0),
        name="adjoint",
    )(*parts, weights, id_rows, choice, places, held)


def rows_to_planes(rows, out_ref):
    low = lower_half(48)
    for m in range(2):
        for q in range(4):
            one = rows[96 * q : 96 * q + 48, 128 * m : 128 * m + 128]
            two = rows[96 * q + 48 : 96 * q + 96, 128 * m : 128 * m + 128]
            even, odd = pair_halves(one, two, low)
            out_ref[2 * m, q] = even
            out_ref[2 * m + 1, q] = odd


def edge_rows(planes_ref, place, z):
    for n in range(NB):
        for q in range(4):
            rows = planes_ref[n, q, pl.ds(z, 6, stride=8), :]
            place[n * 6 : n * 6 + 6, 128 * q : 128 * q + 128] = rows


def images_kernel(
    own_ref, plus_ref, minus_ref, planes_ref, low_ref, high_ref, rows
):
    sensor, last = lax.axis_index("sensor"), 7
    keep_low = jnp.where(sensor > 0, 1.0, 0.0).astype(F32)
    keep_high = jnp.where(sensor < last, 1.0, 0.0).astype(F32)
    for h in range(8):
        block = slice(32 * h, 32 * h + 32)
        rows[48 * h : 48 * h + 8, :] = plus_ref[block, :].astype(F32)[24:32] * keep_low
        rows[48 * h + 8 : 48 * h + 40, :] = own_ref[block, :].astype(F32)
        rows[48 * h + 40 : 48 * h + 48, :] = minus_ref[block, :].astype(F32)[0:8] * keep_high
    rows_to_planes(rows, planes_ref)
    edge_rows(planes_ref, low_ref, 0)
    edge_rows(planes_ref, high_ref, 7)


def images(shards):
    return pl.pallas_call(
        images_kernel,
        out_shape=[
            jax.ShapeDtypeStruct((NB, 4, 48, 128), F32),
            jax.ShapeDtypeStruct((24, 512), F32),
            jax.ShapeDtypeStruct((24, 512), F32),
        ],
        in_specs=[vmem()] * len(shards),
        out_specs=[vmem()] * 3,
        scratch_shapes=[pltpu.VMEM((384, 256), F32)],
        compiler_params=params(16),
        cost_estimate=cost(0.7),
        name="images_to_planes",
    )(*shards)


def add_scattered(acc, contrib):
    coded = contrib[SLOTS:SENT, :].astype(F32)
    ids = (coded[0:2] * 16.0 + coded[2:4]).astype(I32)
    x = (ids >> 6) - 4 * lax.axis_index("sensor") + 1
    index = (ids & 7) * 48 + x * 8 + ((ids >> 3) & 7)
    index = jnp.where((x >= 0) & (x < 6), index, -1)
    first = lax.broadcasted_iota(I32, (384, 256), 0)
    second = lax.broadcasted_iota(I32, (384, SLOTS - 256), 0)
    hot = jnp.where(first == index[0:1, :], 1.0, 0.0).astype(BF16)
    more = jnp.where(second == index[1:2, 0 : SLOTS - 256], 1.0, 0.0).astype(BF16)
    acc = acc + jnp.dot(hot, contrib[0:256, :], preferred_element_type=F32)
    return acc + jnp.dot(more, contrib[256:SLOTS, :], preferred_element_type=F32)


def write_planes(acc, image_low_ref, image_high_ref, planes_ref, inner_ref, outer_ref, rows, low, high):
    rows[...] = acc
    rows_to_planes(rows, planes_ref)
    low[0:24, :] = image_low_ref[...]
    high[0:24, :] = image_high_ref[...]
    edge_rows(planes_ref, low.at[pl.ds(24, 24)], 0)
    edge_rows(planes_ref, high.at[pl.ds(24, 24)], 7)
    first_core = lax.rem(lax.axis_index("slab"), 2) == 0
    inner_ref[...] = jnp.where(first_core, high[...], low[...]).astype(BF16)
    outer_ref[...] = jnp.where(first_core, low[...], high[...]).astype(BF16)


PLANES = [
    jax.ShapeDtypeStruct((NB, 4, 48, 128), F32),
    jax.ShapeDtypeStruct((48, 512), BF16),
    jax.ShapeDtypeStruct((48, 512), BF16),
]
PLANE_SCRATCH = [
    pltpu.VMEM((384, 256), F32),
    pltpu.VMEM((48, 512), F32),
    pltpu.VMEM((48, 512), F32),
]


def packed_kernel(*refs):
    packed, (low_in, high_in, planes_ref, inner_ref, outer_ref, over_ref) = refs[:8], refs[8:14]
    acc = jnp.zeros((384, 256), F32)
    row = lax.broadcasted_iota(I32, (384, CAP), 0)
    over = jnp.zeros((8, 256), F32)
    for ref in packed:
        coded = ref[CAP:PACKED, :].astype(F32)
        over = jnp.maximum(over, coded[8:16])
        place = (coded[0:1] * 16.0 + coded[1:2]).astype(I32)
        place = jnp.where(coded[2:3] > 0.0, place, -1)[:, 0:CAP]
        hot = jnp.where(row == place, 1.0, 0.0).astype(BF16)
        acc = acc + jnp.dot(hot, ref[0:CAP, :], preferred_element_type=F32)
    over_ref[...] = over[0:1, 0:1].astype(I32)
    write_planes(acc, low_in, high_in, planes_ref, inner_ref, outer_ref, *refs[14:])


def packed_planes(packed, image_low, image_high):
    return pl.pallas_call(
        packed_kernel,
        out_shape=[*PLANES, jax.ShapeDtypeStruct((1, 1), I32)],
        in_specs=[vmem()] * 10,
        out_specs=[vmem()] * 4,
        scratch_shapes=PLANE_SCRATCH,
        compiler_params=params(16),
        cost_estimate=cost(1.5),
        name="gradient_planes",
    )(*packed, image_low, image_high)


def whole_kernel(*refs):
    whole, (half_a_ref, half_b_ref, low_in, high_in) = refs[:7], refs[7:11]
    (planes_ref, inner_ref, outer_ref), far, scratch = refs[11:14], refs[14], refs[15:]
    far[0:SENT_SPLIT, :] = half_a_ref[...]
    far[SENT_SPLIT:SENT, :] = half_b_ref[...]
    acc = jnp.zeros((384, 256), F32)
    for contrib in (*whole, far):
        acc = add_scattered(acc, contrib)
    write_planes(acc, low_in, high_in, planes_ref, inner_ref, outer_ref, *scratch)


def whole_planes(contrib, image_low, image_high):
    two, back = from_sensor(contrib, 2), from_sensor(contrib, -2)
    near = [contrib, from_sensor(contrib, 1), from_sensor(contrib, -1), two, back]
    far = spread_far(two, back, SENT_SPLIT)
    return pl.pallas_call(
        whole_kernel,
        out_shape=PLANES,
        in_specs=[vmem()] * 11,
        out_specs=[vmem()] * 3,
        scratch_shapes=[pltpu.VMEM((SENT, 256), BF16), *PLANE_SCRATCH],
        compiler_params=params(16),
        cost_estimate=cost(2.0),
        name="gradient_planes_whole",
    )(*near, *far, image_low, image_high)


def shifted_rows(rows, e):
    if e == 1:
        return rows
    y = lax.broadcasted_iota(I32, rows.shape, 1)
    if e == 0:
        return jnp.where(y == 0, 0.0, pltpu.roll(rows, 1, axis=1))
    return jnp.where(y == 511, 0.0, pltpu.roll(rows, 511, axis=1))


def conv_kernel(
    image_ref, grad_ref, inner_ref, outer_ref, matrix_ref, out_w_ref, out_ref,
    body, ends, done,
):
    first_core = lax.rem(lax.axis_index("slab"), 2) == 0
    inner, outer = inner_ref[...].astype(F32), outer_ref[...].astype(F32)
    below, above = jnp.where(first_core, outer, inner), jnp.where(first_core, inner, outer)
    for kind, (edge, start) in enumerate(((below, 0), (above, 0), (below, 24), (above, 24))):
        rows = edge[start : start + 24]
        for e in range(3):
            moved = shifted_rows(rows, e)
            for q in range(4):
                ends[q, pl.ds(kind + 4 * e, 24, stride=16), :] = moved[:, 128 * q : 128 * q + 128]
    for q in range(4):
        ends[q, pl.ds(12, 24, stride=16), :] = jnp.ones((24, 128), F32)
        for r in range(13, 16):
            ends[q, pl.ds(r, 24, stride=16), :] = jnp.zeros((24, 128), F32)
    for n in range(NB):
        for x in range(6):
            rows = jnp.concatenate(
                [
                    jnp.concatenate([ref[n, q, 8 * x : 8 * x + 8, :] for q in range(4)], axis=1)
                    for ref in (image_ref, grad_ref)
                ],
                axis=0,
            )
            for e in range(3):
                body[e, n * 6 + x] = shifted_rows(rows, e).astype(BF16)

    def one_x(x, carry):
        for n in range(NB):
            for half in range(2):
                cols = slice(256 * half, 256 * half + 256)
                tiles = [body[e, n * 6 + x + a, :, cols] for a in range(3) for e in range(3)]
                for a in range(3):
                    at = pl.multiple_of((n * 6 + x + a) * 16, 16)
                    pair = [ends[2 * half + q, pl.ds(at, 16), :] for q in range(2)]
                    tiles.append(jnp.concatenate(pair, axis=1).astype(BF16))
                stack = jnp.concatenate(tiles, axis=0)
                hidden = jnp.dot(matrix_ref[0], stack, preferred_element_type=F32)
                hidden = hidden + jnp.dot(matrix_ref[1], stack, preferred_element_type=F32)
                at = pl.multiple_of(8 * x + 8, 8)
                pair = [image_ref[n, 2 * half + q, pl.ds(at, 8), :] for q in range(2)]
                total = jnp.concatenate(pair, axis=1)
                for c in range(CHAN):
                    total = total + jnp.maximum(hidden[8 * c : 8 * c + 8], 0.0) * out_w_ref[c]
                for q in range(2):
                    part = total[:, 128 * q : 128 * q + 128]
                    done[2 * half + q, pl.ds(n, 8, stride=4), :] = part
        for z in range(8):
            for q in range(4):
                out_ref[x, z, :, 128 * q : 128 * q + 128] = done[q, 4 * z : 4 * z + 4, :]
        return carry

    lax.fori_loop(0, 4, one_x, 0)


def convolve(image, grad, inner, outer, matrix, out_w):
    return pl.pallas_call(
        conv_kernel,
        out_shape=jax.ShapeDtypeStruct((4, 8, NB, 512), F32),
        in_specs=[vmem()] * 5 + [smem()],
        out_specs=vmem(),
        scratch_shapes=[
            pltpu.VMEM((3, 24, 16, 512), BF16),
            pltpu.VMEM((4, 384, 128), F32),
            pltpu.VMEM((4, 32, 128), F32),
        ],
        compiler_params=params(32),
        cost_estimate=cost(5.0),
        name="convolutions",
    )(image, grad, inner, outer, matrix, out_w)


def tap_choice():
    choice = np.zeros((55, 8, TAPS), np.float32)
    for z in range(8):
        for a in range(3):
            for e in range(3):
                for i in range(2):
                    for plane in range(-1, 9):
                        b = plane - z + 1
                        if not 0 <= b <= 2:
                            continue
                        if 0 <= plane < 8:
                            column = (a * 3 + e) * 16 + i * 8 + plane
                        else:
                            column = 144 + a * 16 + i * 2 + (plane > 0) + 4 * e
                        choice[i * 27 + (a * 3 + b) * 3 + e, z, column] = 1.0
        choice[54, z, 144 + 12] = 1.0
    return choice


def conv_matrix(conv_in, conv_bias):
    table = jnp.concatenate([conv_in.reshape(CHAN, 54), conv_bias[:, None]], axis=1)
    high = lax.reduce_precision(table, 8, 7)
    parts = jnp.concatenate([high, table - high], axis=0).astype(BF16)
    choice = jnp.asarray(tap_choice().reshape(55, 8 * TAPS), BF16)
    spread = jnp.dot(parts, choice, preferred_element_type=F32).astype(BF16)
    return spread.reshape(2, CHAN * 8, TAPS)


def ring(distance, count):
    return [(i, (i + distance) % count) for i in range(count)]


def slab_perm(dy, dx, core):
    def index(y, x, c):
        return (y % 4 * 4 + x % 4) * 2 + c

    return [
        (index(y, x, c), index(y + dy, x + dx, c ^ core))
        for y in range(4)
        for x in range(4)
        for c in range(2)
    ]


def from_sensor(block, distance):
    return lax.ppermute(block, "sensor", ring(distance, 8))


def spread_far(plus, minus, split):
    return [
        from_sensor(plus, 1),
        from_sensor(minus, -1),
        from_sensor(plus[:split], 2),
        from_sensor(minus[split:], -2),
    ]


def chip_sum(partial):
    other = lax.ppermute(partial, "slab", slab_perm(0, 0, 1))
    total = partial.astype(F32) + other.astype(F32)
    return total.astype(BF16)


def slab_sum_parts(total):
    moved = [lax.ppermute(total, "slab", slab_perm(0, d, 0)) for d in (1, 3, 2)]
    row = total.astype(F32) + moved[0].astype(F32) + moved[1].astype(F32) + moved[2].astype(F32)
    row = row.astype(BF16)
    return [row] + [lax.ppermute(row, "slab", slab_perm(d, 0, 0)) for d in (1, 3, 2)]


def slot_weights(live_slots, exponents):
    slot_iota = lax.broadcasted_iota(I32, exponents.shape, 1)
    scaled = jnp.exp2(exponents.astype(F32))
    return jnp.where(slot_iota < live_slots[:, None], scaled, jnp.zeros_like(scaled))


def on_device(volume, measured, blocks, voxel_ids, counts, exponents, conv_in, conv_bias, conv_out):
    ids = voxel_ids.T.reshape(SLOTS)
    padded = jnp.pad(ids, (0, 512 - SLOTS), constant_values=4080).reshape(2, 256)
    id_rows = jnp.concatenate([padded >> 4, padded & 15, jnp.zeros((12, 256), I32)], axis=0)
    keys = (ids & ~255) | ((ids & 7) << 5) | ((ids >> 3) & 31)
    keys = keys.reshape(SLOTS, 1)
    weights = slot_weights(counts[:, 0], exponents).T.reshape(SLOTS, 1)
    stacked = blocks.reshape(JB, KS * 64, TB)

    plus, minus = from_sensor(volume, 1), from_sensor(volume, -1)
    two, back = from_sensor(volume, 2), from_sensor(volume, -2)
    far = spread_far(two, back, 2)
    held = hold(stacked, two)
    before, *near = gather_first(keys, weights, [volume, plus, minus, two, back])
    partial = project(
        keys, weights, before, far, measured, held
    )
    chip = chip_sum(partial)
    held = hold(stacked, chip)
    parts = slab_sum_parts(chip)
    matrix = conv_matrix(conv_in, conv_bias)
    image, image_low, image_high = images(near)
    live_row = weights.reshape(1, SLOTS)
    choice, places = plan(ids.reshape(1, SLOTS), live_row)
    contrib, *packed = adjoint(parts, weights, id_rows.astype(BF16), choice, places, held)
    moved = [packed[0]] + [from_sensor(packed[d % 8], d) for d in (4, 3, -3, 2, -2, 1, -1)]
    grad, inner, outer, over = packed_planes(moved, image_low, image_high)
    grad, inner, outer = lax.cond(
        over[0, 0] > 0,
        lambda: tuple(whole_planes(contrib, image_low, image_high)),
        lambda: (grad, inner, outer),
    )
    inner = lax.ppermute(inner, "slab", slab_perm(0, 0, 1))
    pairs = [(2 * i + 1, 2 * i + 2) for i in range(15)]
    outer = lax.ppermute(outer, "slab", pairs + [(b, a) for a, b in pairs])
    return convolve(image, grad, inner, outer, matrix, conv_out)


def solution(mesh):
    in_specs = (
        P("sensor", "slab", None, None),
        P(("sensor", "slab"), None, None),
        P("sensor", "slab", None, None),
        P("sensor", "slab"),
        P("sensor", "slab"),
        P("sensor", "slab"),
        P(),
        P(),
        P(),
    )
    out_specs = P("sensor", "slab", None, None)
    return jax.shard_map(
        on_device, mesh=mesh, in_specs=in_specs, out_specs=out_specs, check_vma=False
    )
```

```python
import functools

import jax
import jax.numpy as jnp
import numpy as np
from jax import lax
from jax.experimental import pallas as pl
from jax.experimental.pallas import tpu as pltpu
from jax.sharding import PartitionSpec as P

F32 = jnp.float32
BF16 = jnp.bfloat16
I32 = jnp.int32

JB = 64
KS = 5
SLOTS = JB * KS
NB = 4
TB = 128
OWN = 256
CAP = 80
PACKED = CAP + 16
SENT = SLOTS + 16
SENT_SPLIT = 176
CHAN = 32
TAPS = 192


def owner_base(step):
    return lax.rem(lax.axis_index("sensor") + (step + 8), 8) * OWN


STEPS = (0, -1, 1, -2, 2, -3, 3, 4)


def vmem():
    return pl.BlockSpec(memory_space=pltpu.VMEM)


def smem():
    return pl.BlockSpec(memory_space=pltpu.SMEM)


def params(mib):
    return pltpu.CompilerParams(vmem_limit_bytes=mib * 1024 * 1024)


def cost(us):
    return pl.CostEstimate(flops=0, bytes_accessed=int(us * 3.0e6), transcendentals=0)


def lower_half(rows):
    return lax.broadcasted_iota(I32, (rows, 128), 1) < 64


def swapped(tile):
    return pltpu.roll(tile, 64, axis=1)


def pair_halves(first, second, low):
    return jnp.where(low, first, swapped(second)), jnp.where(low, swapped(first), second)


def planes_to_rows(volume_refs, rows, out_ref):
    i = 0
    for volume_ref in volume_refs:
        for x in range(volume_ref.shape[0]):
            for z in range(8):
                image = volume_ref[x, z].astype(F32)
                for q in range(4):
                    rows[q, 4 * i : 4 * i + 4, :] = image[:, 128 * q : 128 * q + 128]
                i += 1
    low = lower_half(32)
    for m in range(2):
        for q in range(4):
            one = rows[q, pl.ds(2 * m, 32, stride=4), :]
            two = rows[q, pl.ds(2 * m + 1, 32, stride=4), :]
            even, odd = pair_halves(one, two, low)
            out_ref[64 * q : 64 * q + 32, 128 * m : 128 * m + 128] = even.astype(BF16)
            out_ref[64 * q + 32 : 64 * q + 64, 128 * m : 128 * m + 128] = odd.astype(BF16)


def add_gathered(acc, keys, weights, base, shard):
    lane = lax.broadcasted_iota(I32, (SLOTS, OWN), 1)
    hot = jnp.where(lane == keys - base, weights, 0.0).astype(BF16)
    return acc + jnp.dot(hot, shard, preferred_element_type=F32)


def gather_kernel(
    keys_ref, weights_ref, own_ref, plus_ref, minus_ref, two_ref, back_ref,
    out_ref, own_rows, plus_rows, minus_rows, rows, shard,
):
    acc = jnp.zeros((SLOTS, 256), F32)
    keys, weights = keys_ref[...], weights_ref[...]
    shards = (own_rows, plus_rows, minus_rows, shard.at[0], shard.at[1])
    for i, ref in enumerate((own_ref, plus_ref, minus_ref, two_ref, back_ref)):
        planes_to_rows([ref], rows.at[i], shards[i])
        acc = add_gathered(acc, keys, weights, owner_base(STEPS[i]), shards[i][...])
    out_ref[...] = acc


def gather_first(keys, weights, shards):
    return pl.pallas_call(
        gather_kernel,
        out_shape=[jax.ShapeDtypeStruct((SLOTS, 256), F32)]
        + [jax.ShapeDtypeStruct((OWN, 256), BF16)] * 3,
        in_specs=[vmem()] * (2 + len(shards)),
        out_specs=[vmem()] * 4,
        scratch_shapes=[
            pltpu.VMEM((5, 4, 128, 128), F32),
            pltpu.VMEM((2, OWN, 256), BF16),
        ],
        compiler_params=params(16),
        cost_estimate=cost(1.5),
        name="gather_first",
    )(keys, weights, *shards)


CHUNKS = 8


def hold_kernel(start, blocks_ref, after_ref, held_ref, sems):
    step = held_ref.shape[0] // CHUNKS
    copies = [
        pltpu.make_async_copy(
            blocks_ref.at[pl.ds(start + c * step, step)],
            held_ref.at[pl.ds(c * step, step)],
            sems.at[c],
        )
        for c in range(CHUNKS)
    ]
    for copy in copies:
        copy.start()
    for copy in copies:
        copy.wait()


def hold(blocks, after, start=0, count=JB):
    return pl.pallas_call(
        functools.partial(hold_kernel, start),
        out_shape=jax.ShapeDtypeStruct((count, KS * 64, TB), BF16),
        in_specs=[pl.BlockSpec(memory_space=pl.ANY), pl.BlockSpec(memory_space=pl.ANY)],
        out_specs=vmem(),
        scratch_shapes=[pltpu.SemaphoreType.DMA((CHUNKS,))],
        compiler_params=params(46),
        cost_estimate=cost(2.5 * count / JB),
        name="hold_blocks",
    )(blocks, after)


def project_kernel(
    keys_ref,
    weights_ref,
    before_ref,
    three_ref,
    minus_ref,
    half_a_ref,
    half_b_ref,
    measured_ref,
    held,
    out_ref,
    rows,
    shard,
    lhs,
    total,
):
    acc = before_ref[...]
    keys, weights = keys_ref[...], weights_ref[...]
    for i, refs in enumerate(((three_ref,), (minus_ref,), (half_a_ref, half_b_ref))):
        planes_to_rows(refs, rows.at[i], shard.at[i])
        acc = add_gathered(acc, keys, weights, owner_base(STEPS[5 + i]), shard[i])
    low = lower_half(JB)
    for m in range(2):
        cols = slice(128 * m, 128 * m + 128)
        for q in range(3):
            one = acc[2 * q * JB : (2 * q + 1) * JB, cols]
            if q < 2:
                two = acc[(2 * q + 1) * JB : (2 * q + 2) * JB, cols]
                even, odd = pair_halves(one, two, low)
            else:
                even, odd = one, swapped(one)
            lhs[q, pl.ds(2 * m, JB, stride=4), :] = even
            lhs[q, pl.ds(2 * m + 1, JB, stride=4), :] = odd
    upper = lax.broadcasted_iota(I32, (8, TB), 0) < 4
    for p in range(JB // 2):
        at = slice(8 * p, 8 * p + 8)
        left = jnp.concatenate([lhs[0, at], lhs[1, at], lhs[2, at, 0:64]], axis=1).astype(BF16)
        both = jnp.concatenate([held[2 * p], held[2 * p + 1]], axis=1)
        got = jnp.dot(left, both, preferred_element_type=F32)
        total[8 * p : 8 * p + 8, :] = jnp.where(upper, got[:, :TB], got[:, TB:])
    mine = pl.ds(pl.multiple_of(lax.axis_index("slab") * 8, 8), 8)
    own = jnp.concatenate([measured_ref[0].astype(F32), measured_ref[1].astype(F32)], axis=0)
    total[mine, :] = total[mine, :] - own
    out_ref[...] = total[...].astype(BF16)


def project(keys, weights, before, rest, measured, held):
    return pl.pallas_call(
        project_kernel,
        out_shape=jax.ShapeDtypeStruct((JB * NB, TB), BF16),
        in_specs=[vmem()] * 9,
        out_specs=vmem(),
        scratch_shapes=[
            pltpu.VMEM((3, 4, 128, 128), F32),
            pltpu.VMEM((3, OWN, 256), BF16),
            pltpu.VMEM((3, JB * NB, 128), F32),
            pltpu.VMEM((JB * NB, TB), F32),
        ],
        compiler_params=params(16),
        cost_estimate=cost(4.0),
        name="project",
    )(keys, weights, before, *rest, measured, held)


def plan_kernel(ids_ref, weights_ref, choice_ref, places_ref):
    sensor = lax.axis_index("sensor")
    ids = jnp.broadcast_to(ids_ref[...], (8, SLOTS))
    live = jnp.broadcast_to(weights_ref[...], (8, SLOTS)) > 0.0
    step = lax.broadcasted_iota(I32, (8, SLOTS), 0)
    owner = lax.rem(sensor + step, 8)
    x = (ids >> 6) - 4 * owner + 1
    needed = live & (x >= 0) & (x < 6)
    place = (ids & 7) * 48 + x * 8 + ((ids >> 3) & 7)
    flags = jnp.where(needed, 1.0, 0.0)
    row = lax.broadcasted_iota(I32, (SLOTS, SLOTS), 0)
    column = lax.broadcasted_iota(I32, (SLOTS, SLOTS), 1)
    before = jnp.where(row < column, 1.0, 0.0).astype(BF16)
    rank = jnp.dot(flags.astype(BF16), before, preferred_element_type=F32)
    high = (place >> 4).astype(F32)
    low = (place & 15).astype(F32)
    most = jnp.max(jnp.sum(flags, axis=1, keepdims=True), axis=0, keepdims=True)
    over = jnp.where(most > CAP, 1.0, 0.0)
    want = lax.broadcasted_iota(I32, (CAP, SLOTS), 0).astype(F32)
    fill = jnp.zeros((4, SLOTS), F32)
    for d in range(8):
        at = slice(d, d + 1)
        rank_d = jnp.where(flags[at] > 0.0, rank[at], -1.0)
        hot = jnp.where(want == rank_d, 1.0, 0.0).astype(BF16)
        choice_ref[d * CAP : (d + 1) * CAP, :] = hot
        values = jnp.concatenate([high[at], low[at], flags[at], flags[at], fill], axis=0)
        coded = lax.dot_general(
            values.astype(BF16), hot, (((1,), (1,)), ((), ())), preferred_element_type=F32
        )
        coded = jnp.concatenate([coded, jnp.zeros((8, CAP), F32) + over], axis=0)
        wide = jnp.concatenate([coded, jnp.zeros((16, 128 - CAP), F32)], axis=1)
        wide = jnp.concatenate([wide, jnp.zeros((16, 128), F32)], axis=1)
        places_ref[d] = wide.astype(BF16)


def plan(ids, weights):
    return pl.pallas_call(
        plan_kernel,
        out_shape=[
            jax.ShapeDtypeStruct((8 * CAP, SLOTS), BF16),
            jax.ShapeDtypeStruct((8, 16, 256), BF16),
        ],
        in_specs=[vmem()] * 2,
        out_specs=[vmem()] * 2,
        compiler_params=params(16),
        cost_estimate=cost(1.5),
        name="plan_sends",
    )(ids, weights)


def adjoint_kernel(
    own_ref, one_ref, two_ref, three_ref, weights_ref, ids_ref, choice_ref, places_ref, held,
    out_ref, *refs,
):
    packed_refs, (resid, back) = refs[:8], refs[8:]
    back[2] = jnp.zeros((JB * NB, 128), F32)
    total = own_ref[...].astype(F32) + one_ref[...].astype(F32)
    total = total + two_ref[...].astype(F32) + three_ref[...].astype(F32)
    resid[...] = total.astype(BF16).astype(F32)
    upper = lax.broadcasted_iota(I32, (8, KS * 64), 0) < 4
    dims = (((1,), (1,)), ((), ()))
    for p in range(JB // 2):
        left = resid[8 * p : 8 * p + 8, :].astype(BF16)
        a = lax.dot_general(left, held[2 * p], dims, preferred_element_type=F32)
        b = lax.dot_general(left, held[2 * p + 1], dims, preferred_element_type=F32)
        got = jnp.where(upper, a, b)
        at = slice(8 * p, 8 * p + 8)
        back[0, at, :] = got[:, 0:128]
        back[1, at, :] = got[:, 128:256]
        back[2, at, 0:64] = got[:, 256 : KS * 64]
    low = lower_half(JB)
    for m in range(2):
        for q in range(3):
            one = back[q, pl.ds(2 * m, JB, stride=4), :]
            two = back[q, pl.ds(2 * m + 1, JB, stride=4), :]
            even, odd = pair_halves(one, two, low)
            for k, part in ((2 * q, even), (2 * q + 1, odd)):
                if k < KS:
                    scaled = part * weights_ref[k * JB : (k + 1) * JB, :]
                    out_ref[k * JB : (k + 1) * JB, 128 * m : 128 * m + 128] = scaled.astype(BF16)
    out_ref[SLOTS:SENT, :] = ids_ref[...]
    rows = out_ref[0:SLOTS, :]
    packed = jnp.dot(choice_ref[...], rows, preferred_element_type=F32).astype(BF16)
    for d, packed_ref in enumerate(packed_refs):
        packed_ref[0:CAP, :] = packed[d * CAP : (d + 1) * CAP]
        packed_ref[CAP:PACKED, :] = places_ref[d]


def adjoint(parts, weights, id_rows, choice, places, held):
    return pl.pallas_call(
        adjoint_kernel,
        out_shape=[jax.ShapeDtypeStruct((SENT, 256), BF16)]
        + [jax.ShapeDtypeStruct((PACKED, 256), BF16)] * 8,
        in_specs=[vmem()] * 9,
        out_specs=[vmem()] * 9,
        scratch_shapes=[
            pltpu.VMEM((JB * NB, TB), F32),
            pltpu.VMEM((3, JB * NB, 128), F32),
        ],
        compiler_params=params(16),
        cost_estimate=cost(3.0),
        name="adjoint",
    )(*parts, weights, id_rows, choice, places, held)


def rows_to_planes(rows, out_ref):
    low = lower_half(48)
    for m in range(2):
        for q in range(4):
            one = rows[96 * q : 96 * q + 48, 128 * m : 128 * m + 128]
            two = rows[96 * q + 48 : 96 * q + 96, 128 * m : 128 * m + 128]
            even, odd = pair_halves(one, two, low)
            out_ref[2 * m, q] = even
            out_ref[2 * m + 1, q] = odd


def edge_rows(planes_ref, place, z):
    for n in range(NB):
        for q in range(4):
            rows = planes_ref[n, q, pl.ds(z, 6, stride=8), :]
            place[n * 6 : n * 6 + 6, 128 * q : 128 * q + 128] = rows


def images_kernel(
    own_ref, plus_ref, minus_ref, planes_ref, low_ref, high_ref, rows
):
    sensor, last = lax.axis_index("sensor"), 7
    keep_low = jnp.where(sensor > 0, 1.0, 0.0).astype(F32)
    keep_high = jnp.where(sensor < last, 1.0, 0.0).astype(F32)
    for h in range(8):
        block = slice(32 * h, 32 * h + 32)
        rows[48 * h : 48 * h + 8, :] = plus_ref[block, :].astype(F32)[24:32] * keep_low
        rows[48 * h + 8 : 48 * h + 40, :] = own_ref[block, :].astype(F32)
        rows[48 * h + 40 : 48 * h + 48, :] = minus_ref[block, :].astype(F32)[0:8] * keep_high
    rows_to_planes(rows, planes_ref)
    edge_rows(planes_ref, low_ref, 0)
    edge_rows(planes_ref, high_ref, 7)


def images(shards):
    return pl.pallas_call(
        images_kernel,
        out_shape=[
            jax.ShapeDtypeStruct((NB, 4, 48, 128), F32),
            jax.ShapeDtypeStruct((24, 512), F32),
            jax.ShapeDtypeStruct((24, 512), F32),
        ],
        in_specs=[vmem()] * len(shards),
        out_specs=[vmem()] * 3,
        scratch_shapes=[pltpu.VMEM((384, 256), F32)],
        compiler_params=params(16),
        cost_estimate=cost(0.7),
        name="images_to_planes",
    )(*shards)


def add_scattered(acc, contrib):
    coded = contrib[SLOTS:SENT, :].astype(F32)
    ids = (coded[0:2] * 16.0 + coded[2:4]).astype(I32)
    x = (ids >> 6) - 4 * lax.axis_index("sensor") + 1
    index = (ids & 7) * 48 + x * 8 + ((ids >> 3) & 7)
    index = jnp.where((x >= 0) & (x < 6), index, -1)
    first = lax.broadcasted_iota(I32, (384, 256), 0)
    second = lax.broadcasted_iota(I32, (384, SLOTS - 256), 0)
    hot = jnp.where(first == index[0:1, :], 1.0, 0.0).astype(BF16)
    more = jnp.where(second == index[1:2, 0 : SLOTS - 256], 1.0, 0.0).astype(BF16)
    acc = acc + jnp.dot(hot, contrib[0:256, :], preferred_element_type=F32)
    return acc + jnp.dot(more, contrib[256:SLOTS, :], preferred_element_type=F32)


def write_planes(acc, image_low_ref, image_high_ref, planes_ref, inner_ref, outer_ref, rows, low, high):
    rows[...] = acc
    rows_to_planes(rows, planes_ref)
    low[0:24, :] = image_low_ref[...]
    high[0:24, :] = image_high_ref[...]
    edge_rows(planes_ref, low.at[pl.ds(24, 24)], 0)
    edge_rows(planes_ref, high.at[pl.ds(24, 24)], 7)
    first_core = lax.rem(lax.axis_index("slab"), 2) == 0
    inner_ref[...] = jnp.where(first_core, high[...], low[...]).astype(BF16)
    outer_ref[...] = jnp.where(first_core, low[...], high[...]).astype(BF16)


PLANES = [
    jax.ShapeDtypeStruct((NB, 4, 48, 128), F32),
    jax.ShapeDtypeStruct((48, 512), BF16),
    jax.ShapeDtypeStruct((48, 512), BF16),
]
PLANE_SCRATCH = [
    pltpu.VMEM((384, 256), F32),
    pltpu.VMEM((48, 512), F32),
    pltpu.VMEM((48, 512), F32),
]


def packed_kernel(*refs):
    packed, (low_in, high_in, planes_ref, inner_ref, outer_ref, over_ref) = refs[:8], refs[8:14]
    acc = jnp.zeros((384, 256), F32)
    row = lax.broadcasted_iota(I32, (384, CAP), 0)
    over = jnp.zeros((8, 256), F32)
    for ref in packed:
        coded = ref[CAP:PACKED, :].astype(F32)
        over = jnp.maximum(over, coded[8:16])
        place = (coded[0:1] * 16.0 + coded[1:2]).astype(I32)
        place = jnp.where(coded[2:3] > 0.0, place, -1)[:, 0:CAP]
        hot = jnp.where(row == place, 1.0, 0.0).astype(BF16)
        acc = acc + jnp.dot(hot, ref[0:CAP, :], preferred_element_type=F32)
    over_ref[...] = over[0:1, 0:1].astype(I32)
    write_planes(acc, low_in, high_in, planes_ref, inner_ref, outer_ref, *refs[14:])


def packed_planes(packed, image_low, image_high):
    return pl.pallas_call(
        packed_kernel,
        out_shape=[*PLANES, jax.ShapeDtypeStruct((1, 1), I32)],
        in_specs=[vmem()] * 10,
        out_specs=[vmem()] * 4,
        scratch_shapes=PLANE_SCRATCH,
        compiler_params=params(16),
        cost_estimate=cost(1.5),
        name="gradient_planes",
    )(*packed, image_low, image_high)


def whole_kernel(*refs):
    whole, (half_a_ref, half_b_ref, low_in, high_in) = refs[:7], refs[7:11]
    (planes_ref, inner_ref, outer_ref), far, scratch = refs[11:14], refs[14], refs[15:]
    far[0:SENT_SPLIT, :] = half_a_ref[...]
    far[SENT_SPLIT:SENT, :] = half_b_ref[...]
    acc = jnp.zeros((384, 256), F32)
    for contrib in (*whole, far):
        acc = add_scattered(acc, contrib)
    write_planes(acc, low_in, high_in, planes_ref, inner_ref, outer_ref, *scratch)


def whole_planes(contrib, image_low, image_high):
    two, back = from_sensor(contrib, 2), from_sensor(contrib, -2)
    near = [contrib, from_sensor(contrib, 1), from_sensor(contrib, -1), two, back]
    far = spread_far(two, back, SENT_SPLIT)
    return pl.pallas_call(
        whole_kernel,
        out_shape=PLANES,
        in_specs=[vmem()] * 11,
        out_specs=[vmem()] * 3,
        scratch_shapes=[pltpu.VMEM((SENT, 256), BF16), *PLANE_SCRATCH],
        compiler_params=params(16),
        cost_estimate=cost(2.0),
        name="gradient_planes_whole",
    )(*near, *far, image_low, image_high)


def shifted_rows(rows, e):
    if e == 1:
        return rows
    y = lax.broadcasted_iota(I32, rows.shape, 1)
    if e == 0:
        return jnp.where(y == 0, 0.0, pltpu.roll(rows, 1, axis=1))
    return jnp.where(y == 511, 0.0, pltpu.roll(rows, 511, axis=1))


def conv_kernel(
    image_ref, grad_ref, inner_ref, outer_ref, matrix_ref, out_w_ref, out_ref,
    body, ends, done,
):
    first_core = lax.rem(lax.axis_index("slab"), 2) == 0
    inner, outer = inner_ref[...].astype(F32), outer_ref[...].astype(F32)
    below, above = jnp.where(first_core, outer, inner), jnp.where(first_core, inner, outer)
    for kind, (edge, start) in enumerate(((below, 0), (above, 0), (below, 24), (above, 24))):
        rows = edge[start : start + 24]
        for e in range(3):
            moved = shifted_rows(rows, e)
            for q in range(4):
                ends[q, pl.ds(kind + 4 * e, 24, stride=16), :] = moved[:, 128 * q : 128 * q + 128]
    for q in range(4):
        ends[q, pl.ds(12, 24, stride=16), :] = jnp.ones((24, 128), F32)
        for r in range(13, 16):
            ends[q, pl.ds(r, 24, stride=16), :] = jnp.zeros((24, 128), F32)
    for n in range(NB):
        for x in range(6):
            rows = jnp.concatenate(
                [
                    jnp.concatenate([ref[n, q, 8 * x : 8 * x + 8, :] for q in range(4)], axis=1)
                    for ref in (image_ref, grad_ref)
                ],
                axis=0,
            )
            for e in range(3):
                body[e, n * 6 + x] = shifted_rows(rows, e).astype(BF16)

    def one_x(x, carry):
        for n in range(NB):
            for half in range(2):
                cols = slice(256 * half, 256 * half + 256)
                tiles = [body[e, n * 6 + x + a, :, cols] for a in range(3) for e in range(3)]
                for a in range(3):
                    at = pl.multiple_of((n * 6 + x + a) * 16, 16)
                    pair = [ends[2 * half + q, pl.ds(at, 16), :] for q in range(2)]
                    tiles.append(jnp.concatenate(pair, axis=1).astype(BF16))
                stack = jnp.concatenate(tiles, axis=0)
                hidden = jnp.dot(matrix_ref[0], stack, preferred_element_type=F32)
                hidden = hidden + jnp.dot(matrix_ref[1], stack, preferred_element_type=F32)
                at = pl.multiple_of(8 * x + 8, 8)
                pair = [image_ref[n, 2 * half + q, pl.ds(at, 8), :] for q in range(2)]
                total = jnp.concatenate(pair, axis=1)
                for c in range(CHAN):
                    total = total + jnp.maximum(hidden[8 * c : 8 * c + 8], 0.0) * out_w_ref[c]
                for q in range(2):
                    part = total[:, 128 * q : 128 * q + 128]
                    done[2 * half + q, pl.ds(n, 8, stride=4), :] = part
        for z in range(8):
            for q in range(4):
                out_ref[x, z, :, 128 * q : 128 * q + 128] = done[q, 4 * z : 4 * z + 4, :]
        return carry

    lax.fori_loop(0, 4, one_x, 0, unroll=True)


def convolve(image, grad, inner, outer, matrix, out_w):
    return pl.pallas_call(
        conv_kernel,
        out_shape=jax.ShapeDtypeStruct((4, 8, NB, 512), F32),
        in_specs=[vmem()] * 5 + [smem()],
        out_specs=vmem(),
        scratch_shapes=[
            pltpu.VMEM((3, 24, 16, 512), BF16),
            pltpu.VMEM((4, 384, 128), F32),
            pltpu.VMEM((4, 32, 128), F32),
        ],
        compiler_params=params(32),
        cost_estimate=cost(5.0),
        name="convolutions",
    )(image, grad, inner, outer, matrix, out_w)


def tap_choice():
    choice = np.zeros((55, 8, TAPS), np.float32)
    for z in range(8):
        for a in range(3):
            for e in range(3):
                for i in range(2):
                    for plane in range(-1, 9):
                        b = plane - z + 1
                        if not 0 <= b <= 2:
                            continue
                        if 0 <= plane < 8:
                            column = (a * 3 + e) * 16 + i * 8 + plane
                        else:
                            column = 144 + a * 16 + i * 2 + (plane > 0) + 4 * e
                        choice[i * 27 + (a * 3 + b) * 3 + e, z, column] = 1.0
        choice[54, z, 144 + 12] = 1.0
    return choice


def conv_matrix(conv_in, conv_bias):
    table = jnp.concatenate([conv_in.reshape(CHAN, 54), conv_bias[:, None]], axis=1)
    high = lax.reduce_precision(table, 8, 7)
    parts = jnp.concatenate([high, table - high], axis=0).astype(BF16)
    choice = jnp.asarray(tap_choice().reshape(55, 8 * TAPS), BF16)
    spread = jnp.dot(parts, choice, preferred_element_type=F32).astype(BF16)
    return spread.reshape(2, CHAN * 8, TAPS)


def ring(distance, count):
    return [(i, (i + distance) % count) for i in range(count)]


def slab_perm(dy, dx, core):
    def index(y, x, c):
        return (y % 4 * 4 + x % 4) * 2 + c

    return [
        (index(y, x, c), index(y + dy, x + dx, c ^ core))
        for y in range(4)
        for x in range(4)
        for c in range(2)
    ]


def from_sensor(block, distance):
    return lax.ppermute(block, "sensor", ring(distance, 8))


def spread_far(plus, minus, split):
    return [
        from_sensor(plus, 1),
        from_sensor(minus, -1),
        from_sensor(plus[:split], 2),
        from_sensor(minus[split:], -2),
    ]


def chip_sum(partial):
    other = lax.ppermute(partial, "slab", slab_perm(0, 0, 1))
    total = partial.astype(F32) + other.astype(F32)
    return total.astype(BF16)


def slab_sum_parts(total):
    moved = [lax.ppermute(total, "slab", slab_perm(0, d, 0)) for d in (1, 3, 2)]
    row = total.astype(F32) + moved[0].astype(F32) + moved[1].astype(F32) + moved[2].astype(F32)
    row = row.astype(BF16)
    return [row] + [lax.ppermute(row, "slab", slab_perm(d, 0, 0)) for d in (1, 3, 2)]


def slot_weights(live_slots, exponents):
    slot_iota = lax.broadcasted_iota(I32, exponents.shape, 1)
    scaled = jnp.exp2(exponents.astype(F32))
    return jnp.where(slot_iota < live_slots[:, None], scaled, jnp.zeros_like(scaled))


def on_device(volume, measured, blocks, voxel_ids, counts, exponents, conv_in, conv_bias, conv_out):
    ids = voxel_ids.T.reshape(SLOTS)
    padded = jnp.pad(ids, (0, 512 - SLOTS), constant_values=4080).reshape(2, 256)
    id_rows = jnp.concatenate([padded >> 4, padded & 15, jnp.zeros((12, 256), I32)], axis=0)
    keys = (ids & ~255) | ((ids & 7) << 5) | ((ids >> 3) & 31)
    keys = keys.reshape(SLOTS, 1)
    weights = slot_weights(counts[:, 0], exponents).T.reshape(SLOTS, 1)
    stacked = blocks.reshape(JB, KS * 64, TB)

    plus, minus = from_sensor(volume, 1), from_sensor(volume, -1)
    two, back = from_sensor(volume, 2), from_sensor(volume, -2)
    far = spread_far(two, back, 2)
    held = hold(stacked, two)
    before, *near = gather_first(keys, weights, [volume, plus, minus, two, back])
    partial = project(
        keys, weights, before, far, measured, held
    )
    chip = chip_sum(partial)
    held = hold(stacked, chip)
    parts = slab_sum_parts(chip)
    matrix = conv_matrix(conv_in, conv_bias)
    image, image_low, image_high = images(near)
    live_row = weights.reshape(1, SLOTS)
    choice, places = plan(ids.reshape(1, SLOTS), live_row)
    contrib, *packed = adjoint(parts, weights, id_rows.astype(BF16), choice, places, held)
    moved = [packed[0]] + [from_sensor(packed[d % 8], d) for d in (4, 3, -3, 2, -2, 1, -1)]
    grad, inner, outer, over = packed_planes(moved, image_low, image_high)
    grad, inner, outer = lax.cond(
        over[0, 0] > 0,
        lambda: tuple(whole_planes(contrib, image_low, image_high)),
        lambda: (grad, inner, outer),
    )
    inner = lax.ppermute(inner, "slab", slab_perm(0, 0, 1))
    pairs = [(2 * i + 1, 2 * i + 2) for i in range(15)]
    outer = lax.ppermute(outer, "slab", pairs + [(b, a) for a, b in pairs])
    return convolve(image, grad, inner, outer, matrix, conv_out)


def solution(mesh):
    in_specs = (
        P("sensor", "slab", None, None),
        P(("sensor", "slab"), None, None),
        P("sensor", "slab", None, None),
        P("sensor", "slab"),
        P("sensor", "slab"),
        P("sensor", "slab"),
        P(),
        P(),
        P(),
    )
    out_specs = P("sensor", "slab", None, None)
    return jax.shard_map(
        on_device, mesh=mesh, in_specs=in_specs, out_specs=out_specs, check_vma=False
    )
```

```python
import functools

import jax
import jax.numpy as jnp
import numpy as np
from jax import lax
from jax.experimental import pallas as pl
from jax.experimental.pallas import tpu as pltpu
from jax.sharding import PartitionSpec as P

F32 = jnp.float32
BF16 = jnp.bfloat16
I32 = jnp.int32

JB = 64
KS = 5
SLOTS = JB * KS
NB = 4
TB = 128
OWN = 256
CAP = 80
PACKED = CAP + 16
SENT = SLOTS + 16
SENT_SPLIT = 176
CHAN = 32
TAPS = 192


def owner_base(step):
    return lax.rem(lax.axis_index("sensor") + (step + 8), 8) * OWN


STEPS = (0, -1, 1, -2, 2, -3, 3, 4)


def vmem():
    return pl.BlockSpec(memory_space=pltpu.VMEM)


def smem():
    return pl.BlockSpec(memory_space=pltpu.SMEM)


def params(mib):
    return pltpu.CompilerParams(vmem_limit_bytes=mib * 1024 * 1024)


def cost(us):
    return pl.CostEstimate(flops=0, bytes_accessed=int(us * 3.0e6), transcendentals=0)


def lower_half(rows):
    return lax.broadcasted_iota(I32, (rows, 128), 1) < 64


def swapped(tile):
    return pltpu.roll(tile, 64, axis=1)


def pair_halves(first, second, low):
    return jnp.where(low, first, swapped(second)), jnp.where(low, swapped(first), second)


def planes_to_rows(volume_refs, rows, out_ref):
    i = 0
    for volume_ref in volume_refs:
        for x in range(volume_ref.shape[0]):
            for z in range(8):
                image = volume_ref[x, z].astype(F32)
                for q in range(4):
                    rows[q, 4 * i : 4 * i + 4, :] = image[:, 128 * q : 128 * q + 128]
                i += 1
    low = lower_half(32)
    for m in range(2):
        for q in range(4):
            one = rows[q, pl.ds(2 * m, 32, stride=4), :]
            two = rows[q, pl.ds(2 * m + 1, 32, stride=4), :]
            even, odd = pair_halves(one, two, low)
            out_ref[64 * q : 64 * q + 32, 128 * m : 128 * m + 128] = even.astype(BF16)
            out_ref[64 * q + 32 : 64 * q + 64, 128 * m : 128 * m + 128] = odd.astype(BF16)


def add_gathered(acc, keys, weights, base, shard):
    lane = lax.broadcasted_iota(I32, (SLOTS, OWN), 1)
    hot = jnp.where(lane == keys - base, weights, 0.0).astype(BF16)
    return acc + jnp.dot(hot, shard, preferred_element_type=F32)


def gather_kernel(
    keys_ref, weights_ref, own_ref, plus_ref, minus_ref, two_ref, back_ref,
    out_ref, own_rows, plus_rows, minus_rows, rows, shard,
):
    acc = jnp.zeros((SLOTS, 256), F32)
    keys, weights = keys_ref[...], weights_ref[...]
    shards = (own_rows, plus_rows, minus_rows, shard.at[0], shard.at[1])
    for i, ref in enumerate((own_ref, plus_ref, minus_ref, two_ref, back_ref)):
        planes_to_rows([ref], rows.at[i], shards[i])
        acc = add_gathered(acc, keys, weights, owner_base(STEPS[i]), shards[i][...])
    out_ref[...] = acc


def gather_first(keys, weights, shards):
    return pl.pallas_call(
        gather_kernel,
        out_shape=[jax.ShapeDtypeStruct((SLOTS, 256), F32)]
        + [jax.ShapeDtypeStruct((OWN, 256), BF16)] * 3,
        in_specs=[vmem()] * (2 + len(shards)),
        out_specs=[vmem()] * 4,
        scratch_shapes=[
            pltpu.VMEM((5, 4, 128, 128), F32),
            pltpu.VMEM((2, OWN, 256), BF16),
        ],
        compiler_params=params(16),
        cost_estimate=cost(1.5),
        name="gather_first",
    )(keys, weights, *shards)


CHUNKS = 8


def hold_kernel(start, blocks_ref, after_ref, held_ref, sems):
    step = held_ref.shape[0] // CHUNKS
    copies = [
        pltpu.make_async_copy(
            blocks_ref.at[pl.ds(start + c * step, step)],
            held_ref.at[pl.ds(c * step, step)],
            sems.at[c],
        )
        for c in range(CHUNKS)
    ]
    for copy in copies:
        copy.start()
    for copy in copies:
        copy.wait()


def hold(blocks, after, start=0, count=JB):
    return pl.pallas_call(
        functools.partial(hold_kernel, start),
        out_shape=jax.ShapeDtypeStruct((count, KS * 64, TB), BF16),
        in_specs=[pl.BlockSpec(memory_space=pl.ANY), pl.BlockSpec(memory_space=pl.ANY)],
        out_specs=vmem(),
        scratch_shapes=[pltpu.SemaphoreType.DMA((CHUNKS,))],
        compiler_params=params(46),
        cost_estimate=cost(2.5 * count / JB),
        name="hold_blocks",
    )(blocks, after)


def project_kernel(
    keys_ref,
    weights_ref,
    before_ref,
    three_ref,
    minus_ref,
    half_a_ref,
    half_b_ref,
    measured_ref,
    held,
    out_ref,
    rows,
    shard,
    lhs,
    total,
):
    acc = before_ref[...]
    keys, weights = keys_ref[...], weights_ref[...]
    for i, refs in enumerate(((three_ref,), (minus_ref,), (half_a_ref, half_b_ref))):
        planes_to_rows(refs, rows.at[i], shard.at[i])
        acc = add_gathered(acc, keys, weights, owner_base(STEPS[5 + i]), shard[i])
    low = lower_half(JB)
    for m in range(2):
        cols = slice(128 * m, 128 * m + 128)
        for q in range(3):
            one = acc[2 * q * JB : (2 * q + 1) * JB, cols]
            if q < 2:
                two = acc[(2 * q + 1) * JB : (2 * q + 2) * JB, cols]
                even, odd = pair_halves(one, two, low)
            else:
                even, odd = one, swapped(one)
            lhs[q, pl.ds(2 * m, JB, stride=4), :] = even
            lhs[q, pl.ds(2 * m + 1, JB, stride=4), :] = odd
    upper = lax.broadcasted_iota(I32, (8, TB), 0) < 4
    for p in range(JB // 2):
        at = slice(8 * p, 8 * p + 8)
        left = jnp.concatenate([lhs[0, at], lhs[1, at], lhs[2, at, 0:64]], axis=1).astype(BF16)
        both = jnp.concatenate([held[2 * p], held[2 * p + 1]], axis=1)
        got = jnp.dot(left, both, preferred_element_type=F32)
        total[8 * p : 8 * p + 8, :] = jnp.where(upper, got[:, :TB], got[:, TB:])
    mine = pl.ds(pl.multiple_of(lax.axis_index("slab") * 8, 8), 8)
    own = jnp.concatenate([measured_ref[0].astype(F32), measured_ref[1].astype(F32)], axis=0)
    total[mine, :] = total[mine, :] - own
    out_ref[...] = total[...].astype(BF16)


def project(keys, weights, before, rest, measured, held):
    return pl.pallas_call(
        project_kernel,
        out_shape=jax.ShapeDtypeStruct((JB * NB, TB), BF16),
        in_specs=[vmem()] * 9,
        out_specs=vmem(),
        scratch_shapes=[
            pltpu.VMEM((3, 4, 128, 128), F32),
            pltpu.VMEM((3, OWN, 256), BF16),
            pltpu.VMEM((3, JB * NB, 128), F32),
            pltpu.VMEM((JB * NB, TB), F32),
        ],
        compiler_params=params(16),
        cost_estimate=cost(4.0),
        name="project",
    )(keys, weights, before, *rest, measured, held)


def plan_kernel(ids_ref, weights_ref, choice_ref, places_ref):
    sensor = lax.axis_index("sensor")
    ids = jnp.broadcast_to(ids_ref[...], (8, SLOTS))
    live = jnp.broadcast_to(weights_ref[...], (8, SLOTS)) > 0.0
    step = lax.broadcasted_iota(I32, (8, SLOTS), 0)
    owner = lax.rem(sensor + step, 8)
    x = (ids >> 6) - 4 * owner + 1
    needed = live & (x >= 0) & (x < 6)
    place = (ids & 7) * 48 + x * 8 + ((ids >> 3) & 7)
    flags = jnp.where(needed, 1.0, 0.0)
    row = lax.broadcasted_iota(I32, (SLOTS, SLOTS), 0)
    column = lax.broadcasted_iota(I32, (SLOTS, SLOTS), 1)
    before = jnp.where(row < column, 1.0, 0.0).astype(BF16)
    rank = jnp.dot(flags.astype(BF16), before, preferred_element_type=F32)
    high = (place >> 4).astype(F32)
    low = (place & 15).astype(F32)
    most = jnp.max(jnp.sum(flags, axis=1, keepdims=True), axis=0, keepdims=True)
    over = jnp.where(most > CAP, 1.0, 0.0)
    want = lax.broadcasted_iota(I32, (CAP, SLOTS), 0).astype(F32)
    fill = jnp.zeros((4, SLOTS), F32)
    for d in range(8):
        at = slice(d, d + 1)
        rank_d = jnp.where(flags[at] > 0.0, rank[at], -1.0)
        hot = jnp.where(want == rank_d, 1.0, 0.0).astype(BF16)
        choice_ref[d * CAP : (d + 1) * CAP, :] = hot
        values = jnp.concatenate([high[at], low[at], flags[at], flags[at], fill], axis=0)
        coded = lax.dot_general(
            values.astype(BF16), hot, (((1,), (1,)), ((), ())), preferred_element_type=F32
        )
        coded = jnp.concatenate([coded, jnp.zeros((8, CAP), F32) + over], axis=0)
        wide = jnp.concatenate([coded, jnp.zeros((16, 128 - CAP), F32)], axis=1)
        wide = jnp.concatenate([wide, jnp.zeros((16, 128), F32)], axis=1)
        places_ref[d] = wide.astype(BF16)


def plan(ids, weights):
    return pl.pallas_call(
        plan_kernel,
        out_shape=[
            jax.ShapeDtypeStruct((8 * CAP, SLOTS), BF16),
            jax.ShapeDtypeStruct((8, 16, 256), BF16),
        ],
        in_specs=[vmem()] * 2,
        out_specs=[vmem()] * 2,
        compiler_params=params(16),
        cost_estimate=cost(1.5),
        name="plan_sends",
    )(ids, weights)


def adjoint_kernel(
    own_ref, one_ref, two_ref, three_ref, weights_ref, ids_ref, choice_ref, places_ref, held,
    out_ref, *refs,
):
    packed_refs, (resid, back) = refs[:8], refs[8:]
    back[2] = jnp.zeros((JB * NB, 128), F32)
    total = own_ref[...].astype(F32) + one_ref[...].astype(F32)
    total = total + two_ref[...].astype(F32) + three_ref[...].astype(F32)
    resid[...] = total.astype(BF16).astype(F32)
    upper = lax.broadcasted_iota(I32, (8, KS * 64), 0) < 4
    dims = (((1,), (1,)), ((), ()))
    for p in range(JB // 2):
        left = resid[8 * p : 8 * p + 8, :].astype(BF16)
        a = lax.dot_general(left, held[2 * p], dims, preferred_element_type=F32)
        b = lax.dot_general(left, held[2 * p + 1], dims, preferred_element_type=F32)
        got = jnp.where(upper, a, b)
        at = slice(8 * p, 8 * p + 8)
        back[0, at, :] = got[:, 0:128]
        back[1, at, :] = got[:, 128:256]
        back[2, at, 0:64] = got[:, 256 : KS * 64]
    low = lower_half(JB)
    for m in range(2):
        for q in range(3):
            one = back[q, pl.ds(2 * m, JB, stride=4), :]
            two = back[q, pl.ds(2 * m + 1, JB, stride=4), :]
            even, odd = pair_halves(one, two, low)
            for k, part in ((2 * q, even), (2 * q + 1, odd)):
                if k < KS:
                    scaled = part * weights_ref[k * JB : (k + 1) * JB, :]
                    out_ref[k * JB : (k + 1) * JB, 128 * m : 128 * m + 128] = scaled.astype(BF16)
    out_ref[SLOTS:SENT, :] = ids_ref[...]
    rows = out_ref[0:SLOTS, :]
    packed = jnp.dot(choice_ref[...], rows, preferred_element_type=F32).astype(BF16)
    for d, packed_ref in enumerate(packed_refs):
        packed_ref[0:CAP, :] = packed[d * CAP : (d + 1) * CAP]
        packed_ref[CAP:PACKED, :] = places_ref[d]


def adjoint(parts, weights, id_rows, choice, places, held):
    return pl.pallas_call(
        adjoint_kernel,
        out_shape=[jax.ShapeDtypeStruct((SENT, 256), BF16)]
        + [jax.ShapeDtypeStruct((PACKED, 256), BF16)] * 8,
        in_specs=[vmem()] * 9,
        out_specs=[vmem()] * 9,
        scratch_shapes=[
            pltpu.VMEM((JB * NB, TB), F32),
            pltpu.VMEM((3, JB * NB, 128), F32),
        ],
        compiler_params=params(16),
        cost_estimate=cost(3.0),
        name="adjoint",
    )(*parts, weights, id_rows, choice, places, held)


def rows_to_planes(rows, out_ref):
    low = lower_half(48)
    for m in range(2):
        for q in range(4):
            one = rows[96 * q : 96 * q + 48, 128 * m : 128 * m + 128]
            two = rows[96 * q + 48 : 96 * q + 96, 128 * m : 128 * m + 128]
            even, odd = pair_halves(one, two, low)
            out_ref[2 * m, q] = even
            out_ref[2 * m + 1, q] = odd


def edge_rows(planes_ref, place, z):
    for n in range(NB):
        for q in range(4):
            rows = planes_ref[n, q, pl.ds(z, 6, stride=8), :]
            place[n * 6 : n * 6 + 6, 128 * q : 128 * q + 128] = rows


def images_kernel(
    own_ref, plus_ref, minus_ref, planes_ref, low_ref, high_ref, rows
):
    sensor, last = lax.axis_index("sensor"), 7
    keep_low = jnp.where(sensor > 0, 1.0, 0.0).astype(F32)
    keep_high = jnp.where(sensor < last, 1.0, 0.0).astype(F32)
    for h in range(8):
        block = slice(32 * h, 32 * h + 32)
        rows[48 * h : 48 * h + 8, :] = plus_ref[block, :].astype(F32)[24:32] * keep_low
        rows[48 * h + 8 : 48 * h + 40, :] = own_ref[block, :].astype(F32)
        rows[48 * h + 40 : 48 * h + 48, :] = minus_ref[block, :].astype(F32)[0:8] * keep_high
    rows_to_planes(rows, planes_ref)
    edge_rows(planes_ref, low_ref, 0)
    edge_rows(planes_ref, high_ref, 7)


def images(shards):
    return pl.pallas_call(
        images_kernel,
        out_shape=[
            jax.ShapeDtypeStruct((NB, 4, 48, 128), F32),
            jax.ShapeDtypeStruct((24, 512), F32),
            jax.ShapeDtypeStruct((24, 512), F32),
        ],
        in_specs=[vmem()] * len(shards),
        out_specs=[vmem()] * 3,
        scratch_shapes=[pltpu.VMEM((384, 256), F32)],
        compiler_params=params(16),
        cost_estimate=cost(0.7),
        name="images_to_planes",
    )(*shards)


def add_scattered(acc, contrib):
    coded = contrib[SLOTS:SENT, :].astype(F32)
    ids = (coded[0:2] * 16.0 + coded[2:4]).astype(I32)
    x = (ids >> 6) - 4 * lax.axis_index("sensor") + 1
    index = (ids & 7) * 48 + x * 8 + ((ids >> 3) & 7)
    index = jnp.where((x >= 0) & (x < 6), index, -1)
    first = lax.broadcasted_iota(I32, (384, 256), 0)
    second = lax.broadcasted_iota(I32, (384, SLOTS - 256), 0)
    hot = jnp.where(first == index[0:1, :], 1.0, 0.0).astype(BF16)
    more = jnp.where(second == index[1:2, 0 : SLOTS - 256], 1.0, 0.0).astype(BF16)
    acc = acc + jnp.dot(hot, contrib[0:256, :], preferred_element_type=F32)
    return acc + jnp.dot(more, contrib[256:SLOTS, :], preferred_element_type=F32)


def write_planes(acc, image_low_ref, image_high_ref, planes_ref, inner_ref, outer_ref, rows, low, high):
    rows[...] = acc
    rows_to_planes(rows, planes_ref)
    low[0:24, :] = image_low_ref[...]
    high[0:24, :] = image_high_ref[...]
    edge_rows(planes_ref, low.at[pl.ds(24, 24)], 0)
    edge_rows(planes_ref, high.at[pl.ds(24, 24)], 7)
    first_core = lax.rem(lax.axis_index("slab"), 2) == 0
    inner_ref[...] = jnp.where(first_core, high[...], low[...]).astype(BF16)
    outer_ref[...] = jnp.where(first_core, low[...], high[...]).astype(BF16)


PLANES = [
    jax.ShapeDtypeStruct((NB, 4, 48, 128), F32),
    jax.ShapeDtypeStruct((48, 512), BF16),
    jax.ShapeDtypeStruct((48, 512), BF16),
]
PLANE_SCRATCH = [
    pltpu.VMEM((384, 256), F32),
    pltpu.VMEM((48, 512), F32),
    pltpu.VMEM((48, 512), F32),
]


def packed_kernel(*refs):
    packed, (low_in, high_in, planes_ref, inner_ref, outer_ref, over_ref) = refs[:8], refs[8:14]
    acc = jnp.zeros((384, 256), F32)
    row = lax.broadcasted_iota(I32, (384, CAP), 0)
    over = jnp.zeros((8, 256), F32)
    for ref in packed:
        coded = ref[CAP:PACKED, :].astype(F32)
        over = jnp.maximum(over, coded[8:16])
        place = (coded[0:1] * 16.0 + coded[1:2]).astype(I32)
        place = jnp.where(coded[2:3] > 0.0, place, -1)[:, 0:CAP]
        hot = jnp.where(row == place, 1.0, 0.0).astype(BF16)
        acc = acc + jnp.dot(hot, ref[0:CAP, :], preferred_element_type=F32)
    over_ref[...] = over[0:1, 0:1].astype(I32)
    write_planes(acc, low_in, high_in, planes_ref, inner_ref, outer_ref, *refs[14:])


def packed_planes(packed, image_low, image_high):
    return pl.pallas_call(
        packed_kernel,
        out_shape=[*PLANES, jax.ShapeDtypeStruct((1, 1), I32)],
        in_specs=[vmem()] * 10,
        out_specs=[vmem()] * 4,
        scratch_shapes=PLANE_SCRATCH,
        compiler_params=params(16),
        cost_estimate=cost(1.5),
        name="gradient_planes",
    )(*packed, image_low, image_high)


def whole_kernel(*refs):
    whole, (half_a_ref, half_b_ref, low_in, high_in) = refs[:7], refs[7:11]
    (planes_ref, inner_ref, outer_ref), far, scratch = refs[11:14], refs[14], refs[15:]
    far[0:SENT_SPLIT, :] = half_a_ref[...]
    far[SENT_SPLIT:SENT, :] = half_b_ref[...]
    acc = jnp.zeros((384, 256), F32)
    for contrib in (*whole, far):
        acc = add_scattered(acc, contrib)
    write_planes(acc, low_in, high_in, planes_ref, inner_ref, outer_ref, *scratch)


def whole_planes(contrib, image_low, image_high):
    two, back = from_sensor(contrib, 2), from_sensor(contrib, -2)
    near = [contrib, from_sensor(contrib, 1), from_sensor(contrib, -1), two, back]
    far = spread_far(two, back, SENT_SPLIT)
    return pl.pallas_call(
        whole_kernel,
        out_shape=PLANES,
        in_specs=[vmem()] * 11,
        out_specs=[vmem()] * 3,
        scratch_shapes=[pltpu.VMEM((SENT, 256), BF16), *PLANE_SCRATCH],
        compiler_params=params(16),
        cost_estimate=cost(2.0),
        name="gradient_planes_whole",
    )(*near, *far, image_low, image_high)


def shifted_rows(rows, e):
    if e == 1:
        return rows
    y = lax.broadcasted_iota(I32, rows.shape, 1)
    if e == 0:
        return jnp.where(y == 0, 0.0, pltpu.roll(rows, 1, axis=1))
    return jnp.where(y == 511, 0.0, pltpu.roll(rows, 511, axis=1))


def stack_kernel(image_ref, grad_ref, body):
    for n in range(NB):
        for x in range(6):
            rows = jnp.concatenate(
                [
                    jnp.concatenate([ref[n, q, 8 * x : 8 * x + 8, :] for q in range(4)], axis=1)
                    for ref in (image_ref, grad_ref)
                ],
                axis=0,
            )
            for e in range(3):
                body[e, n * 6 + x] = shifted_rows(rows, e).astype(BF16)


def stack_rows(image, grad):
    return pl.pallas_call(
        stack_kernel,
        out_shape=jax.ShapeDtypeStruct((3, 24, 16, 512), BF16),
        in_specs=[vmem()] * 2,
        out_specs=vmem(),
        compiler_params=params(16),
        cost_estimate=cost(1.0),
        name="stack_rows",
    )(image, grad)


def conv_kernel(
    image_ref, body, inner_ref, outer_ref, matrix_ref, out_w_ref, out_ref, ends, done
):
    first_core = lax.rem(lax.axis_index("slab"), 2) == 0
    inner, outer = inner_ref[...].astype(F32), outer_ref[...].astype(F32)
    below, above = jnp.where(first_core, outer, inner), jnp.where(first_core, inner, outer)
    for kind, (edge, start) in enumerate(((below, 0), (above, 0), (below, 24), (above, 24))):
        rows = edge[start : start + 24]
        for e in range(3):
            moved = shifted_rows(rows, e)
            for q in range(4):
                ends[q, pl.ds(kind + 4 * e, 24, stride=16), :] = moved[:, 128 * q : 128 * q + 128]
    for q in range(4):
        ends[q, pl.ds(12, 24, stride=16), :] = jnp.ones((24, 128), F32)
        for r in range(13, 16):
            ends[q, pl.ds(r, 24, stride=16), :] = jnp.zeros((24, 128), F32)

    def one_x(x, carry):
        for n in range(NB):
            for half in range(2):
                cols = slice(256 * half, 256 * half + 256)
                tiles = [body[e, n * 6 + x + a, :, cols] for a in range(3) for e in range(3)]
                for a in range(3):
                    at = pl.multiple_of((n * 6 + x + a) * 16, 16)
                    pair = [ends[2 * half + q, pl.ds(at, 16), :] for q in range(2)]
                    tiles.append(jnp.concatenate(pair, axis=1).astype(BF16))
                stack = jnp.concatenate(tiles, axis=0)
                hidden = jnp.dot(matrix_ref[0], stack, preferred_element_type=F32)
                hidden = hidden + jnp.dot(matrix_ref[1], stack, preferred_element_type=F32)
                at = pl.multiple_of(8 * x + 8, 8)
                pair = [image_ref[n, 2 * half + q, pl.ds(at, 8), :] for q in range(2)]
                total = jnp.concatenate(pair, axis=1)
                for c in range(CHAN):
                    total = total + jnp.maximum(hidden[8 * c : 8 * c + 8], 0.0) * out_w_ref[c]
                for q in range(2):
                    part = total[:, 128 * q : 128 * q + 128]
                    done[2 * half + q, pl.ds(n, 8, stride=4), :] = part
        for z in range(8):
            for q in range(4):
                out_ref[x, z, :, 128 * q : 128 * q + 128] = done[q, 4 * z : 4 * z + 4, :]
        return carry

    lax.fori_loop(0, 4, one_x, 0, unroll=True)


def convolve(image, body, inner, outer, matrix, out_w):
    return pl.pallas_call(
        conv_kernel,
        out_shape=jax.ShapeDtypeStruct((4, 8, NB, 512), F32),
        in_specs=[vmem()] * 5 + [smem()],
        out_specs=vmem(),
        scratch_shapes=[
            pltpu.VMEM((4, 384, 128), F32),
            pltpu.VMEM((4, 32, 128), F32),
        ],
        compiler_params=params(32),
        cost_estimate=cost(5.0),
        name="convolutions",
    )(image, body, inner, outer, matrix, out_w)


def tap_choice():
    choice = np.zeros((55, 8, TAPS), np.float32)
    for z in range(8):
        for a in range(3):
            for e in range(3):
                for i in range(2):
                    for plane in range(-1, 9):
                        b = plane - z + 1
                        if not 0 <= b <= 2:
                            continue
                        if 0 <= plane < 8:
                            column = (a * 3 + e) * 16 + i * 8 + plane
                        else:
                            column = 144 + a * 16 + i * 2 + (plane > 0) + 4 * e
                        choice[i * 27 + (a * 3 + b) * 3 + e, z, column] = 1.0
        choice[54, z, 144 + 12] = 1.0
    return choice


def conv_matrix(conv_in, conv_bias):
    table = jnp.concatenate([conv_in.reshape(CHAN, 54), conv_bias[:, None]], axis=1)
    high = lax.reduce_precision(table, 8, 7)
    parts = jnp.concatenate([high, table - high], axis=0).astype(BF16)
    choice = jnp.asarray(tap_choice().reshape(55, 8 * TAPS), BF16)
    spread = jnp.dot(parts, choice, preferred_element_type=F32).astype(BF16)
    return spread.reshape(2, CHAN * 8, TAPS)


def ring(distance, count):
    return [(i, (i + distance) % count) for i in range(count)]


def slab_perm(dy, dx, core):
    def index(y, x, c):
        return (y % 4 * 4 + x % 4) * 2 + c

    return [
        (index(y, x, c), index(y + dy, x + dx, c ^ core))
        for y in range(4)
        for x in range(4)
        for c in range(2)
    ]


def from_sensor(block, distance):
    return lax.ppermute(block, "sensor", ring(distance, 8))


def spread_far(plus, minus, split):
    return [
        from_sensor(plus, 1),
        from_sensor(minus, -1),
        from_sensor(plus[:split], 2),
        from_sensor(minus[split:], -2),
    ]


def chip_sum(partial):
    other = lax.ppermute(partial, "slab", slab_perm(0, 0, 1))
    total = partial.astype(F32) + other.astype(F32)
    return total.astype(BF16)


def slab_sum_parts(total):
    moved = [lax.ppermute(total, "slab", slab_perm(0, d, 0)) for d in (1, 3, 2)]
    row = total.astype(F32) + moved[0].astype(F32) + moved[1].astype(F32) + moved[2].astype(F32)
    row = row.astype(BF16)
    return [row] + [lax.ppermute(row, "slab", slab_perm(d, 0, 0)) for d in (1, 3, 2)]


def slot_weights(live_slots, exponents):
    slot_iota = lax.broadcasted_iota(I32, exponents.shape, 1)
    scaled = jnp.exp2(exponents.astype(F32))
    return jnp.where(slot_iota < live_slots[:, None], scaled, jnp.zeros_like(scaled))


def on_device(volume, measured, blocks, voxel_ids, counts, exponents, conv_in, conv_bias, conv_out):
    ids = voxel_ids.T.reshape(SLOTS)
    padded = jnp.pad(ids, (0, 512 - SLOTS), constant_values=4080).reshape(2, 256)
    id_rows = jnp.concatenate([padded >> 4, padded & 15, jnp.zeros((12, 256), I32)], axis=0)
    keys = (ids & ~255) | ((ids & 7) << 5) | ((ids >> 3) & 31)
    keys = keys.reshape(SLOTS, 1)
    weights = slot_weights(counts[:, 0], exponents).T.reshape(SLOTS, 1)
    stacked = blocks.reshape(JB, KS * 64, TB)

    plus, minus = from_sensor(volume, 1), from_sensor(volume, -1)
    two, back = from_sensor(volume, 2), from_sensor(volume, -2)
    far = spread_far(two, back, 2)
    held = hold(stacked, two)
    before, *near = gather_first(keys, weights, [volume, plus, minus, two, back])
    partial = project(
        keys, weights, before, far, measured, held
    )
    chip = chip_sum(partial)
    held = hold(stacked, chip)
    parts = slab_sum_parts(chip)
    matrix = conv_matrix(conv_in, conv_bias)
    image, image_low, image_high = images(near)
    live_row = weights.reshape(1, SLOTS)
    choice, places = plan(ids.reshape(1, SLOTS), live_row)
    contrib, *packed = adjoint(parts, weights, id_rows.astype(BF16), choice, places, held)
    moved = [packed[0]] + [from_sensor(packed[d % 8], d) for d in (4, 3, -3, 2, -2, 1, -1)]
    grad, inner, outer, over = packed_planes(moved, image_low, image_high)
    grad, inner, outer = lax.cond(
        over[0, 0] > 0,
        lambda: tuple(whole_planes(contrib, image_low, image_high)),
        lambda: (grad, inner, outer),
    )
    inner = lax.ppermute(inner, "slab", slab_perm(0, 0, 1))
    pairs = [(2 * i + 1, 2 * i + 2) for i in range(15)]
    outer = lax.ppermute(outer, "slab", pairs + [(b, a) for a, b in pairs])
    return convolve(image, stack_rows(image, grad), inner, outer, matrix, conv_out)


def solution(mesh):
    in_specs = (
        P("sensor", "slab", None, None),
        P(("sensor", "slab"), None, None),
        P("sensor", "slab", None, None),
        P("sensor", "slab"),
        P("sensor", "slab"),
        P("sensor", "slab"),
        P(),
        P(),
        P(),
    )
    out_specs = P("sensor", "slab", None, None)
    return jax.shard_map(
        on_device, mesh=mesh, in_specs=in_specs, out_specs=out_specs, check_vma=False
    )
```
